32 devices in a mesh: parts: 2 (over x), wide: 16 (over z, y, core).
Axes of the slice: x: 2, y: 2, z: 4, core: 2. Of those that a mesh axis runs over, the one named last changes fastest.
Arguments:
- tokens: bfloat16 [384, 7168], P(('parts', 'wide')), parts along dimension 0, may hold values from -6 to 6
- expert_ids: int32 [384, 8], P(('parts', 'wide')), parts along dimension 0, may hold values from 0 to 15, as said below
- gates: float32 [384, 8], P(('parts', 'wide')), parts along dimension 0, may hold values from 0.1 to 1
- w_gate: bfloat16 [2, 7168, 8192], P(None, None, 'wide'), may hold values from -0.0625 to 0.0625
- w_up: bfloat16 [2, 7168, 8192], P(None, None, 'wide'), may hold values from -0.0625 to 0.0625
- w_down: bfloat16 [2, 8192, 7168], P(None, 'wide'), may hold values from -0.1875 to 0.1875
Outputs:
- moe_out: bfloat16 [384, 7168], P(('parts', 'wide')), parts along dimension 0
The draws below stay inside these ranges and needn't reach their ends.
There are 2 independent parts, one for each index of `parts`. The reference program is written for one: setup_inputs(seed, part) draws one part's arguments, and reference() takes and returns one part's arrays. A program takes and returns all parts, laid end to end along the dimension named above; an argument that names none is the same for every part. Nothing has to cross between parts.
Inputs may be any that keep to these rules, and one draw needn't show every extreme that they name: `expert_ids`: each row names the 2 experts g * 2 to g * 2 + 1 of each of 4 different groups g, in any order; in each part one group is named by every row.
All inputs are finite; a program needn't handle non-finite values.
Results may differ from the reference program's by a relative error of at most 0.0064.
Values may be sent and summed in bfloat16 or wider, within the bound.
No kernel may reach another device: no remote copies, remote signals or barrier semaphores. Data moves between devices by JAX's collectives and lax.ppermute only.
A program may use at most 128 MiB of HBM per device.

```python
import jax
import jax.numpy as jnp
from jax import lax

D = 7168
GROUPS = 8
TOPG = 4
TOPK = 8
EXP_G = 2
FH = 1024
TOKENS = 192
EXPERTS = 16
N_WIDE = 16


def draw_expert_ids(key, part):
    key_hot, key_group, key_order = jax.random.split(jax.random.fold_in(key, 7103), 3)
    hot_group = jax.random.randint(key_hot, (), 0, GROUPS)
    group_range = jnp.arange(GROUPS, dtype=jnp.int32)
    noise = jax.random.randint(key_group, (TOKENS, GROUPS), 0, 1 << 20)
    scores = noise * GROUPS + group_range[None, :]
    scores = jnp.where(group_range[None, :] == hot_group, -1, scores)
    chosen_groups = jnp.argsort(scores, axis=1, stable=True)[:, :TOPG]
    experts_named = (chosen_groups[:, :, None] * EXP_G + jnp.arange(EXP_G, dtype=jnp.int32)[None, None, :]).reshape(TOKENS, TOPK)
    order_noise = jax.random.randint(key_order, (TOKENS, TOPK), 0, 1 << 20) * TOPK + jnp.arange(TOPK, dtype=jnp.int32)[None, :]
    shuffle = jnp.argsort(order_noise, axis=1, stable=True)
    return jnp.take_along_axis(experts_named, shuffle, axis=1).astype(jnp.int32)


def block_scale(stream_key, dims, cuts, least, top_value):
    factor_of, own = 1.0, jax.random.fold_in(stream_key, 6)
    for axis_at, parts in cuts:
        heights = jnp.exp(jax.random.uniform(jax.random.fold_in(own, axis_at), (parts,), jnp.float32, least / len(cuts), top_value / len(cuts)))
        factor_of = factor_of * jnp.repeat(heights, dims[axis_at] // parts).reshape([-1 if axis == axis_at else 1 for axis in range(len(dims))])
    return factor_of


def centred(key, shape, spread, limit, pieces=(), kind=jnp.bfloat16):
    result = jax.random.normal(key, shape, jnp.float32) * spread
    if len(pieces) > 0:
        result = block_scale(key, shape, pieces, -0.22, 0.18) * result
    return jnp.clip(result, min=-limit, max=limit).astype(kind)


def setup_inputs(seed: int = 0, part: int = 0) -> dict:
    keys = jax.random.split(jax.random.key(seed), 7)
    part_keys = jax.random.split(jax.random.fold_in(keys[6], part), 7)
    return {
        "tokens": centred(part_keys[0], (TOKENS, D), 1.0, 6.0, ((0, 16),)),
        "expert_ids": draw_expert_ids(jax.random.fold_in(jax.random.fold_in(keys[6], part), 71), part),
        "gates": jnp.clip(0.1 + 0.9 * jax.random.uniform(part_keys[2], (TOKENS, TOPK), jnp.float32) ** block_scale(part_keys[2], (TOKENS, TOPK), ((0, 16),), -0.2, 0.2), 0.1, 1.0),
        "w_gate": centred(keys[3], (EXP_G, D, GROUPS * FH), D ** -0.5, 0.0625, ((2, 16),)),
        "w_up": centred(keys[4], (EXP_G, D, GROUPS * FH), D ** -0.5, 0.0625, ((2, 16),)),
        "w_down": centred(keys[5], (EXP_G, GROUPS * FH, D), FH ** -0.5, 0.1875, ((1, 16),)),
    }


def reference(tokens, expert_ids, gates, w_gate, w_up, w_down):
    group_size = N_WIDE // GROUPS
    block_width = FH // group_size
    catalog = jnp.arange(EXPERTS, dtype=jnp.int32)
    picked = expert_ids[:, :, None] == catalog[None, None, :]
    route_weight = jnp.sum(jnp.where(picked, gates[:, :, None], jnp.float32(0.0)), axis=1).astype(jnp.bfloat16)

    def add_block(device, summed):
        device = jnp.asarray(device).astype(jnp.int32)
        group_index = device // group_size
        column_start = (device * block_width).astype(jnp.int32)
        gate_block = lax.dynamic_slice_in_dim(w_gate, column_start, block_width, 2)
        up_block = lax.dynamic_slice_in_dim(w_up, column_start, block_width, 2)
        down_block = lax.dynamic_slice_in_dim(w_down, column_start, block_width, 1)
        scales = lax.dynamic_slice_in_dim(route_weight, (group_index * EXP_G).astype(jnp.int32), EXP_G, 1).astype(jnp.float32)
        partial_value = jnp.zeros((TOKENS, D), jnp.float32)
        for expert in range(EXP_G):
            gate_value = jnp.dot(tokens, gate_block[expert], preferred_element_type=jnp.float32)
            lifted = jnp.dot(tokens, up_block[expert], preferred_element_type=jnp.float32)
            hidden = (jax.nn.silu(gate_value) * lifted).astype(jnp.bfloat16)
            partial_value = partial_value + scales[:, expert:expert + 1] * jnp.dot(hidden, down_block[expert], preferred_element_type=jnp.float32)
        rounded = lax.optimization_barrier(partial_value.astype(jnp.bfloat16))
        return summed + rounded.astype(jnp.float32)

    summed = lax.fori_loop(0, N_WIDE, add_block, jnp.zeros((TOKENS, D), jnp.float32))
    return summed.astype(jnp.bfloat16)
```

```python
import functools

import jax
import jax.numpy as jnp
from jax import lax
from jax.experimental import pallas as pl
from jax.experimental.pallas import tpu as pltpu
from jax.sharding import PartitionSpec as P

GROUPS = 8
EXP_G = 2
LANES = 128
TILE = 8
MIB = 1 << 20
IN_CHUNKS = 4
OUT_CHUNKS = 4
bf16 = jnp.bfloat16
f32 = jnp.float32


def swap(block, bits, count):
    return lax.ppermute(block, "wide", [(i, i ^ bits) for i in range(count)])


def half_roll(block):
    return pltpu.roll(block, TILE // 2, 0)


def low_half(shape):
    return lax.broadcasted_iota(jnp.int32, shape, 0) < TILE // 2


def unpack_pair(u, v):
    full = (u.shape[0] - TILE) // 2
    u_rest, v_rest = u[2 * full :], v[2 * full :]
    low = low_half(u_rest.shape)
    a = [u[:full], v[:full], jnp.where(low, u_rest, half_roll(v_rest))]
    b = [u[full : 2 * full], v[full : 2 * full], jnp.where(low, half_roll(u_rest), v_rest)]
    return a, b


def pack_pair(a, b):
    full = (a.shape[0] - TILE) // 2
    a_rest, b_rest = a[2 * full :], b[2 * full :]
    low = low_half(a_rest.shape)
    u = [a[:full], b[:full], jnp.where(low, a_rest, half_roll(b_rest))]
    v = [a[full : 2 * full], b[full : 2 * full], jnp.where(low, half_roll(a_rest), b_rest)]
    return u, v


def prepare_kernel(chunks, tokens_ref, ids_ref, gates_ref, *refs):
    outs, rows_ref, route_ref = refs[:chunks], refs[chunks], refs[chunks + 1]
    rows, width = tokens_ref.shape
    full = rows // TILE * TILE
    half = width // chunks // 2
    rows_ref[0:rows, :] = tokens_ref[...].astype(f32)
    catalog = lax.broadcasted_iota(jnp.int32, (rows, LANES), 1)
    weight = jnp.zeros((rows, LANES), f32)
    for k in range(ids_ref.shape[1]):
        weight = weight + jnp.where(ids_ref[:, k : k + 1] == catalog, gates_ref[:, k : k + 1], 0.0)
    route_ref[0:rows, :] = weight

    def packed(a_first, b_first, a_rest, b_rest):
        low = low_half(a_rest.shape)
        rest = jnp.where(low, a_rest, half_roll(b_rest))
        return jnp.concatenate([a_first, b_first, rest], 0).astype(bf16)

    for c in range(chunks):
        a = slice(2 * c * half, (2 * c + 1) * half)
        b = slice((2 * c + 1) * half, (2 * c + 2) * half)
        outs[c][:, 0:half] = packed(
            rows_ref[0:full, a], rows_ref[0:full, b], rows_ref[full : full + TILE, a], rows_ref[full : full + TILE, b]
        )
    outs[0][:, half : half + LANES] = packed(
        route_ref[0:full, :],
        jnp.zeros((full, LANES), f32),
        route_ref[full : full + TILE, :],
        jnp.zeros((TILE, LANES), f32),
    )


def prepare(tokens, expert_ids, gates, chunks):
    rows, width = tokens.shape
    half = width // chunks // 2
    padded = -(-rows // TILE) * TILE
    shapes = [jax.ShapeDtypeStruct((2 * rows, half + (LANES if c == 0 else 0)), bf16) for c in range(chunks)]
    return pl.pallas_call(
        functools.partial(prepare_kernel, chunks),
        out_shape=shapes,
        scratch_shapes=[pltpu.VMEM((padded, width), f32), pltpu.VMEM((padded, LANES), f32)],
    )(tokens, expert_ids, gates)


def unpack_rows(refs, half, unit, lhs_ref, route_ref):
    at = 0
    for ref in refs:
        for start in range(0, ref.shape[0], 4 * unit):
            block = ref[start : start + 4 * unit, :].astype(f32)
            pieces_a, pieces_b = [], []
            for pair in range(2):
                u = block[2 * pair * unit : (2 * pair + 1) * unit]
                v = block[(2 * pair + 1) * unit : (2 * pair + 2) * unit]
                a, b = unpack_pair(u, v)
                pieces_a += a
                pieces_b += b
            rows_a = jnp.concatenate(pieces_a, 0)
            count = rows_a.shape[0]
            lhs_ref[at : at + count, 0:half] = rows_a[:, :half].astype(bf16)
            lhs_ref[at : at + count, half : 2 * half] = jnp.concatenate(pieces_b, 0)[:, :half].astype(bf16)
            if route_ref is not None:
                route_ref[at : at + count, :] = rows_a[:, half:]
            at += count


def down_chunk(hidden, weight_ref, half, unit, keep_ref, send_ref):
    rows = hidden.shape[0]
    depth = weight_ref.shape[1]
    total = None
    for expert in range(EXP_G):
        part = jnp.dot(
            hidden[:, expert * depth : (expert + 1) * depth], weight_ref[expert], preferred_element_type=f32
        )
        total = part if total is None else total + part
    blocks = []
    for at in range(0, rows, unit):
        u, v = pack_pair(total[at : at + unit, :half], total[at : at + unit, half:])
        blocks += u + v
    packed = jnp.concatenate(blocks, 0).astype(bf16)
    keep_ref[...] = packed[:rows]
    send_ref[...] = packed[rows:]


def first_kernel(index, half, unit, first, last, *refs):
    refs = list(refs)
    near_ref, next_ref, other_ref = refs[:3]
    refs = refs[3:]
    if first:
        group_ref = refs.pop(0)
    else:
        prior_ref = refs.pop(0)
        if last:
            scale_ref = refs.pop(0)
    gate_ref, up_ref = refs[:2]
    refs = refs[2:]
    if last:
        down_ref, hidden_ref, keep_ref, send_ref = refs[:4]
        refs = refs[4:]
    else:
        acc_ref = refs.pop(0)
        if first:
            scale_ref = refs.pop(0)
    lhs_ref, weights_ref, sems = refs[:3]
    width = 2 * half
    copies = []
    for expert in range(EXP_G):
        for which, source in enumerate((gate_ref, up_ref)):
            copy = pltpu.make_async_copy(
                source.at[expert, pl.ds(index * width, width), :],
                weights_ref.at[expert, which],
                sems.at[2 * expert + which],
            )
            copy.start()
            copies.append(copy)
    if last:
        down_weights_ref, down_sem = refs[3:5]
        down_copy = pltpu.make_async_copy(down_ref.at[:, :, pl.ds(0, down_weights_ref.shape[2])], down_weights_ref, down_sem)
        down_copy.start()
    route_ref = refs[3] if first else None
    unpack_rows((near_ref, next_ref, other_ref), half, unit, lhs_ref, route_ref)
    if first:
        lane = lax.broadcasted_iota(jnp.int32, route_ref.shape, 1)
        for expert in range(EXP_G):
            chosen = jnp.where(lane == group_ref[0] * EXP_G + expert, route_ref[...], 0.0)
            scale_ref[expert] = jnp.broadcast_to(jnp.sum(chosen, 1, keepdims=True), route_ref.shape)
    depth = gate_ref.shape[2]
    hidden = []
    for expert in range(EXP_G):
        parts = []
        for which in range(2):
            copies[2 * expert + which].wait()
            value = jnp.dot(lhs_ref[...], weights_ref[expert, which], preferred_element_type=f32)
            if not first:
                value = value + prior_ref[expert, which]
            if last:
                parts.append(value)
            else:
                acc_ref[expert, which] = value
        if last:
            gate_value, lifted = parts
            value = gate_value / (1.0 + jnp.exp(-gate_value)) * lifted * scale_ref[expert][:, 0:1]
            hidden_ref[:, expert * depth : (expert + 1) * depth] = value.astype(bf16)
    if last:
        down_copy.wait()
        down_chunk(hidden_ref[...], down_weights_ref, down_weights_ref.shape[2] // 2, unit, keep_ref, send_ref)


def expert_step(index, chunks, blocks, extra, w_gate, w_up, w_down, unit, out_chunks):
    first, last = index == 0, index == chunks - 1
    width = w_gate.shape[1] // chunks
    half = width // 2
    depth = w_gate.shape[2]
    rows = sum(b.shape[0] for b in blocks) // 2
    vmem = pl.BlockSpec(memory_space=pltpu.VMEM)
    hbm = pl.BlockSpec(memory_space=pl.ANY)
    smem = pl.BlockSpec(memory_space=pltpu.SMEM)
    scratch = [
        pltpu.VMEM((rows, width), bf16),
        pltpu.VMEM((EXP_G, 2, width, depth), bf16),
        pltpu.SemaphoreType.DMA((2 * EXP_G,)),
    ]
    args, specs = list(blocks), [vmem] * len(blocks)
    args += list(extra)
    specs += [smem] if first else [vmem] * len(extra)
    args += [w_gate, w_up]
    specs += [hbm, hbm]
    bytes_in = EXP_G * 2 * width * depth * 2
    if last:
        columns = w_down.shape[2] // out_chunks
        args.append(w_down)
        specs.append(hbm)
        shapes = [
            jax.ShapeDtypeStruct((rows, EXP_G * depth), bf16),
            jax.ShapeDtypeStruct((rows, columns // 2), bf16),
            jax.ShapeDtypeStruct((rows, columns // 2), bf16),
        ]
        scratch += [pltpu.VMEM((EXP_G, depth, columns), bf16), pltpu.SemaphoreType.DMA]
        bytes_in += EXP_G * depth * columns * 2
    else:
        shapes = [jax.ShapeDtypeStruct((EXP_G, 2, rows, depth), f32)]
        if first:
            shapes.append(jax.ShapeDtypeStruct((EXP_G, rows, LANES), f32))
            scratch.append(pltpu.VMEM((rows, LANES), f32))
    return pl.pallas_call(
        functools.partial(first_kernel, index, half, unit, first, last),
        out_shape=shapes,
        in_specs=specs,
        out_specs=[vmem] * len(shapes),
        scratch_shapes=scratch,
        compiler_params=pltpu.CompilerParams(vmem_limit_bytes=48 * MIB),
        cost_estimate=pl.CostEstimate(flops=rows * bytes_in, bytes_accessed=bytes_in, transcendentals=0),
    )(*args)


def down_kernel(index, half, unit, hidden_ref, down_ref, keep_ref, send_ref, weights_ref, sem):
    columns = 2 * half
    copy = pltpu.make_async_copy(down_ref.at[:, :, pl.ds(index * columns, columns)], weights_ref, sem)
    copy.start()
    copy.wait()
    down_chunk(hidden_ref[...], weights_ref, half, unit, keep_ref, send_ref)


def down_step(index, chunks, hidden, w_down, unit):
    columns = w_down.shape[2] // chunks
    depth = w_down.shape[1]
    rows = hidden.shape[0]
    vmem = pl.BlockSpec(memory_space=pltpu.VMEM)
    bytes_in = EXP_G * depth * columns * 2
    return pl.pallas_call(
        functools.partial(down_kernel, index, columns // 2, unit),
        out_shape=[jax.ShapeDtypeStruct((rows, columns // 2), bf16)] * 2,
        in_specs=[vmem, pl.BlockSpec(memory_space=pl.ANY)],
        out_specs=[vmem] * 2,
        scratch_shapes=[pltpu.VMEM((EXP_G, depth, columns), bf16), pltpu.SemaphoreType.DMA],
        compiler_params=pltpu.CompilerParams(vmem_limit_bytes=48 * MIB),
        cost_estimate=pl.CostEstimate(flops=rows * bytes_in, bytes_accessed=bytes_in, transcendentals=0),
    )(hidden, w_down)


def finish_kernel(chunks, rows, *refs):
    out_ref, whole_ref = refs[-2:]
    refs = refs[:-2]
    per = len(refs) // chunks
    full = rows // TILE * TILE
    half = refs[0].shape[1]
    for c in range(chunks):
        total = refs[c * per][...].astype(f32)
        for ref in refs[c * per + 1 : (c + 1) * per]:
            total = total + ref[...].astype(f32)
        a = slice(2 * c * half, (2 * c + 1) * half)
        b = slice((2 * c + 1) * half, (2 * c + 2) * half)
        rest = total[2 * full :]
        whole_ref[0:full, a] = total[:full]
        whole_ref[0:full, b] = total[full : 2 * full]
        whole_ref[full : full + TILE, a] = rest
        whole_ref[full : full + TILE, b] = half_roll(rest)
    out_ref[...] = whole_ref[0:rows, :].astype(bf16)


def finish(parts, rows, width):
    chunks = len(parts)
    padded = -(-rows // TILE) * TILE
    return pl.pallas_call(
        functools.partial(finish_kernel, chunks, rows),
        out_shape=jax.ShapeDtypeStruct((rows, width), bf16),
        scratch_shapes=[pltpu.VMEM((padded, width), f32)],
    )(*[p for chunk in parts for p in chunk])


def local(tokens, expert_ids, gates, w_gate, w_up, w_down):
    count = lax.axis_size("wide")
    group_size = count // GROUPS
    far = count // 4
    rows, width = tokens.shape
    unit = 2 * rows
    group = (lax.axis_index("wide") // group_size).astype(jnp.int32).reshape(1)
    chunks = prepare(tokens, expert_ids, gates, IN_CHUNKS)

    state = None
    for c, own in enumerate(chunks):
        line = jnp.concatenate([own] + [swap(own, 4 * f, count) for f in range(1, far)], 0)
        crossed = swap(line, 2, count)
        other = swap(jnp.concatenate([line, crossed], 0), 1, count)
        blocks = (line, crossed, other)
        if c == 0:
            extra = [group]
        elif c < IN_CHUNKS - 1:
            extra = [state]
        else:
            extra = [state, scale]
        result = expert_step(c, IN_CHUNKS, blocks, extra, w_gate, w_up, w_down, unit, OUT_CHUNKS)
        if c == 0:
            state, scale = result
        elif c < IN_CHUNKS - 1:
            state = result[0]
    hidden, keep, send = result

    parts = []
    for c in range(OUT_CHUNKS):
        if c > 0:
            keep, send = down_step(c, OUT_CHUNKS, hidden, w_down, unit)
        got = swap(send, 1, count)
        summed = (keep.astype(f32) + got.astype(f32)).astype(bf16)
        middle = summed.shape[0] // 2
        got = swap(summed[middle:], 2, count)
        summed = (summed[:middle].astype(f32) + got.astype(f32)).astype(bf16)
        pieces = [summed[f * unit : (f + 1) * unit] for f in range(far)]
        parts.append([pieces[0]] + [swap(pieces[f], 4 * f, count) for f in range(1, far)])
    return finish(parts, rows, width)


def solution(mesh):
    return jax.shard_map(
        local,
        mesh=mesh,
        in_specs=(
            P(("parts", "wide"), None),
            P(("parts", "wide"), None),
            P(("parts", "wide"), None),
            P(None, None, "wide"),
            P(None, None, "wide"),
            P(None, "wide", None),
        ),
        out_specs=P(("parts", "wide"), None),
        check_vma=False,
    )
```

```python
import functools

import jax
import jax.numpy as jnp
from jax import lax
from jax.experimental import pallas as pl
from jax.experimental.pallas import tpu as pltpu
from jax.sharding import PartitionSpec as P

GROUPS = 8
EXP_G = 2
LANES = 128
TILE = 8
MIB = 1 << 20
IN_SHARES = (1, 1)
OUT_SHARES = (1, 1)
bf16 = jnp.bfloat16
f32 = jnp.float32


def swap(block, bits, count):
    return lax.ppermute(block, "wide", [(i, i ^ bits) for i in range(count)])


def half_roll(block):
    return pltpu.roll(block, TILE // 2, 0)


def low_half(shape):
    return lax.broadcasted_iota(jnp.int32, shape, 0) < TILE // 2


def unpack_pair(u, v):
    full = (u.shape[0] - TILE) // 2
    u_rest, v_rest = u[2 * full :], v[2 * full :]
    low = low_half(u_rest.shape)
    a = [u[:full], v[:full], jnp.where(low, u_rest, half_roll(v_rest))]
    b = [u[full : 2 * full], v[full : 2 * full], jnp.where(low, half_roll(u_rest), v_rest)]
    return a, b


def pack_pair(a, b):
    full = (a.shape[0] - TILE) // 2
    a_rest, b_rest = a[2 * full :], b[2 * full :]
    low = low_half(a_rest.shape)
    u = [a[:full], b[:full], jnp.where(low, a_rest, half_roll(b_rest))]
    v = [a[full : 2 * full], b[full : 2 * full], jnp.where(low, half_roll(a_rest), b_rest)]
    return u, v


def packed(a_first, b_first, a_rest, b_rest):
    low = low_half(a_rest.shape)
    return jnp.concatenate([a_first, b_first, jnp.where(low, a_rest, half_roll(b_rest))], 0).astype(bf16)


def pack_columns(rows_ref, start, half):
    full = rows_ref.shape[0] - TILE
    a, b = slice(start, start + half), slice(start + half, start + 2 * half)
    return packed(rows_ref[:full, a], rows_ref[:full, b], rows_ref[full:, a], rows_ref[full:, b])


def prepare_first_kernel(bounds, tokens_ref, *refs):
    rows_ref = refs[-1]
    rows_ref[0 : tokens_ref.shape[0], :] = tokens_ref[...].astype(f32)
    for out_ref, (start, half) in zip(refs[:-1], bounds, strict=True):
        out_ref[...] = pack_columns(rows_ref, start, half)


def prepare_last_kernel(start, half, tokens_ref, ids_ref, gates_ref, out_ref, rows_ref, route_ref):
    rows = tokens_ref.shape[0]
    rows_ref[0:rows, :] = tokens_ref[...].astype(f32)
    out_ref[:, :half] = pack_columns(rows_ref, start, half)
    experts = GROUPS * EXP_G
    catalog = lax.broadcasted_iota(jnp.int32, (experts, rows), 0)
    weight = jnp.zeros((experts, rows), f32)
    for k in range(ids_ref.shape[0]):
        weight = weight + jnp.where(ids_ref[k : k + 1, :] == catalog, gates_ref[k : k + 1, :], 0.0)
    row = lax.broadcasted_iota(jnp.int32, (experts, LANES), 0)
    eye = (row == lax.broadcasted_iota(jnp.int32, (experts, LANES), 1)).astype(bf16)
    route_ref[0:rows, :] = lax.dot_general(
        weight.astype(bf16), eye, (((0,), (0,)), ((), ())), preferred_element_type=f32
    )
    full = rows // TILE * TILE
    none = jnp.zeros((TILE, LANES), f32)
    out_ref[:, half:] = packed(route_ref[:full, :], jnp.zeros((full, LANES), f32), route_ref[full:, :], none)


def prepare(tokens, expert_ids, gates, bounds):
    rows, width = tokens.shape
    padded = -(-rows // TILE) * TILE
    first = pl.pallas_call(
        functools.partial(prepare_first_kernel, bounds[:-1]),
        out_shape=[jax.ShapeDtypeStruct((2 * rows, half), bf16) for _, half in bounds[:-1]],
        scratch_shapes=[pltpu.VMEM((padded, width), f32)],
    )(tokens)
    start, half = bounds[-1]
    last = pl.pallas_call(
        functools.partial(prepare_last_kernel, start, half),
        out_shape=jax.ShapeDtypeStruct((2 * rows, half + LANES), bf16),
        scratch_shapes=[pltpu.VMEM((padded, width), f32), pltpu.VMEM((padded, LANES), f32)],
    )(tokens, expert_ids.T, gates.T)
    return list(first) + [last]


def cut(width, shares):
    step = 2 * LANES
    blocks = width // step
    ends = [round(blocks * sum(shares[: i + 1]) / sum(shares)) for i in range(len(shares))]
    return [(step * low, LANES * (high - low)) for low, high in zip([0] + ends[:-1], ends, strict=True)]


def unpack_rows(refs, half, unit, lhs_ref, route_ref):
    at = 0
    for ref in refs:
        for start in range(0, ref.shape[0], 4 * unit):
            block = ref[start : start + 4 * unit, :].astype(f32)
            pieces_a, pieces_b = [], []
            for pair in range(2):
                u = block[2 * pair * unit : (2 * pair + 1) * unit]
                v = block[(2 * pair + 1) * unit : (2 * pair + 2) * unit]
                a, b = unpack_pair(u, v)
                pieces_a += a
                pieces_b += b
            rows_a = jnp.concatenate(pieces_a, 0)
            count = rows_a.shape[0]
            lhs_ref[at : at + count, 0:half] = rows_a[:, :half].astype(bf16)
            lhs_ref[at : at + count, half : 2 * half] = jnp.concatenate(pieces_b, 0)[:, :half].astype(bf16)
            if route_ref is not None:
                route_ref[at : at + count, :] = rows_a[:, half:]
            at += count


def down_chunk(hidden, weight_ref, half, unit, keep_ref, send_ref):
    rows = hidden.shape[0]
    depth = weight_ref.shape[1]
    total = None
    for expert in range(EXP_G):
        part = jnp.dot(
            hidden[:, expert * depth : (expert + 1) * depth], weight_ref[expert], preferred_element_type=f32
        )
        total = part if total is None else total + part
    blocks = []
    for at in range(0, rows, unit):
        u, v = pack_pair(total[at : at + unit, :half], total[at : at + unit, half:])
        blocks += u + v
    packed = jnp.concatenate(blocks, 0).astype(bf16)
    keep_ref[...] = packed[:rows]
    send_ref[...] = packed[rows:]


def first_kernel(start, half, unit, first, last, *refs):
    refs = list(refs)
    blocks = refs[:3]
    refs = refs[3:]
    group_ref = refs.pop(0) if last else None
    prior_ref = None if first else refs.pop(0)
    gate_ref, up_ref = refs[:2]
    refs = refs[2:]
    if last:
        down_ref, hidden_ref, keep_ref, send_ref = refs[:4]
        refs = refs[4:]
    else:
        acc_ref = refs.pop(0)
    lhs_ref, weights_ref, sems = refs[:3]
    copies = []
    for expert in range(EXP_G):
        for which, source in enumerate((gate_ref, up_ref)):
            copy = pltpu.make_async_copy(
                source.at[expert, pl.ds(start, 2 * half), :], weights_ref.at[expert, which], sems.at[2 * expert + which]
            )
            copy.start()
            copies.append(copy)
    if last:
        down_weights_ref, down_sem, route_ref = refs[3:6]
        down_copy = pltpu.make_async_copy(
            down_ref.at[:, :, pl.ds(0, down_weights_ref.shape[2])], down_weights_ref, down_sem
        )
        down_copy.start()
    unpack_rows(blocks, half, unit, lhs_ref, route_ref if last else None)
    depth = gate_ref.shape[2]
    if last:
        lane = lax.broadcasted_iota(jnp.int32, route_ref.shape, 1)
    for expert in range(EXP_G):
        parts = []
        for which in range(2):
            copies[2 * expert + which].wait()
            value = jnp.dot(lhs_ref[...], weights_ref[expert, which], preferred_element_type=f32)
            if not first:
                value = value + prior_ref[expert, which]
            if last:
                parts.append(value)
            else:
                acc_ref[expert, which] = value
        if last:
            chosen = jnp.where(lane == group_ref[0] * EXP_G + expert, route_ref[...], 0.0)
            gate_value, lifted = parts
            value = gate_value / (1.0 + jnp.exp(-gate_value)) * lifted * jnp.sum(chosen, 1, keepdims=True)
            hidden_ref[:, expert * depth : (expert + 1) * depth] = value.astype(bf16)
    if last:
        down_copy.wait()
        down_chunk(hidden_ref[...], down_weights_ref, down_weights_ref.shape[2] // 2, unit, keep_ref, send_ref)


def expert_step(bounds, index, blocks, extra, w_gate, w_up, w_down, unit, out_half):
    first, last = index == 0, index == len(bounds) - 1
    start, half = bounds[index]
    width = 2 * half
    depth = w_gate.shape[2]
    rows = sum(b.shape[0] for b in blocks) // 2
    vmem = pl.BlockSpec(memory_space=pltpu.VMEM)
    hbm = pl.BlockSpec(memory_space=pl.ANY)
    smem = pl.BlockSpec(memory_space=pltpu.SMEM)
    scratch = [
        pltpu.VMEM((rows, width), bf16),
        pltpu.VMEM((EXP_G, 2, width, depth), bf16),
        pltpu.SemaphoreType.DMA((2 * EXP_G,)),
    ]
    args = [*blocks, *extra, w_gate, w_up]
    specs = [vmem] * len(blocks) + ([smem] if last else []) + ([] if first else [vmem]) + [hbm, hbm]
    bytes_in = EXP_G * 2 * width * depth * 2
    if last:
        columns = 2 * out_half
        args.append(w_down)
        specs.append(hbm)
        shapes = [jax.ShapeDtypeStruct((rows, EXP_G * depth), bf16)] + [jax.ShapeDtypeStruct((rows, out_half), bf16)] * 2
        scratch += [
            pltpu.VMEM((EXP_G, depth, columns), bf16),
            pltpu.SemaphoreType.DMA,
            pltpu.VMEM((rows, LANES), f32),
        ]
        bytes_in += EXP_G * depth * columns * 2
    else:
        shapes = [jax.ShapeDtypeStruct((EXP_G, 2, rows, depth), f32)]
    return pl.pallas_call(
        functools.partial(first_kernel, start, half, unit, first, last),
        out_shape=shapes,
        in_specs=specs,
        out_specs=[vmem] * len(shapes),
        scratch_shapes=scratch,
        compiler_params=pltpu.CompilerParams(vmem_limit_bytes=48 * MIB),
        cost_estimate=pl.CostEstimate(flops=rows * bytes_in, bytes_accessed=bytes_in, transcendentals=0),
    )(*args)


def down_kernel(start, half, unit, hidden_ref, down_ref, keep_ref, send_ref, weights_ref, sem):
    copy = pltpu.make_async_copy(down_ref.at[:, :, pl.ds(start, 2 * half)], weights_ref, sem)
    copy.start()
    copy.wait()
    down_chunk(hidden_ref[...], weights_ref, half, unit, keep_ref, send_ref)


def down_step(start, half, hidden, w_down, unit):
    depth = w_down.shape[1]
    rows = hidden.shape[0]
    vmem = pl.BlockSpec(memory_space=pltpu.VMEM)
    bytes_in = EXP_G * depth * 2 * half * 2
    return pl.pallas_call(
        functools.partial(down_kernel, start, half, unit),
        out_shape=[jax.ShapeDtypeStruct((rows, half), bf16)] * 2,
        in_specs=[vmem, pl.BlockSpec(memory_space=pl.ANY)],
        out_specs=[vmem] * 2,
        scratch_shapes=[pltpu.VMEM((EXP_G, depth, 2 * half), bf16), pltpu.SemaphoreType.DMA],
        compiler_params=pltpu.CompilerParams(vmem_limit_bytes=48 * MIB),
        cost_estimate=pl.CostEstimate(flops=rows * bytes_in, bytes_accessed=bytes_in, transcendentals=0),
    )(hidden, w_down)


def finish_kernel(bounds, rows, *refs):
    out_ref, whole_ref = refs[-2:]
    refs = refs[:-2]
    per = len(refs) // len(bounds)
    full = rows // TILE * TILE
    for c, (start, half) in enumerate(bounds):
        total = refs[c * per][...].astype(f32)
        for ref in refs[c * per + 1 : (c + 1) * per]:
            total = total + ref[...].astype(f32)
        a, b = slice(start, start + half), slice(start + half, start + 2 * half)
        rest = total[2 * full :]
        whole_ref[:full, a] = total[:full]
        whole_ref[:full, b] = total[full : 2 * full]
        whole_ref[full:, a] = rest
        whole_ref[full:, b] = half_roll(rest)
    out_ref[...] = whole_ref[0:rows, :].astype(bf16)


def finish(parts, bounds, rows, width):
    padded = -(-rows // TILE) * TILE
    return pl.pallas_call(
        functools.partial(finish_kernel, bounds, rows),
        out_shape=jax.ShapeDtypeStruct((rows, width), bf16),
        scratch_shapes=[pltpu.VMEM((padded, width), f32)],
    )(*[p for chunk in parts for p in chunk])


def local(tokens, expert_ids, gates, w_gate, w_up, w_down):
    count = lax.axis_size("wide")
    group_size = count // GROUPS
    far = count // 4
    rows, width = tokens.shape
    unit = 2 * rows
    group = (lax.axis_index("wide") // group_size).astype(jnp.int32).reshape(1)
    bounds = cut(width, IN_SHARES)
    out_bounds = cut(width, OUT_SHARES)
    chunks = prepare(tokens, expert_ids, gates, bounds)

    state = []
    for c, own in enumerate(chunks):
        line = jnp.concatenate([own] + [swap(own, 4 * f, count) for f in range(1, far)], 0)
        crossed = swap(line, 2, count)
        other = swap(jnp.concatenate([line, crossed], 0), 1, count)
        extra = [*([group] if c == len(chunks) - 1 else []), *state]
        state = expert_step(
            bounds, c, (line, crossed, other), extra, w_gate, w_up, w_down, unit, out_bounds[0][1]
        )
    hidden, keep, send = state

    parts = []
    for c, (start, half) in enumerate(out_bounds):
        if c > 0:
            keep, send = down_step(start, half, hidden, w_down, unit)
        got = swap(send, 1, count)
        summed = (keep.astype(f32) + got.astype(f32)).astype(bf16)
        middle = summed.shape[0] // 2
        got = swap(summed[middle:], 2, count)
        summed = (summed[:middle].astype(f32) + got.astype(f32)).astype(bf16)
        pieces = [summed[f * unit : (f + 1) * unit] for f in range(far)]
        parts.append([pieces[0]] + [swap(pieces[f], 4 * f, count) for f in range(1, far)])
    return finish(parts, out_bounds, rows, width)


def solution(mesh):
    return jax.shard_map(
        local,
        mesh=mesh,
        in_specs=(
            P(("parts", "wide"), None),
            P(("parts", "wide"), None),
            P(("parts", "wide"), None),
            P(None, None, "wide"),
            P(None, None, "wide"),
            P(None, "wide", None),
        ),
        out_specs=P(("parts", "wide"), None),
        check_vma=False,
    )
```

```python
import functools

import jax
import jax.numpy as jnp
from jax import lax
from jax.experimental import pallas as pl
from jax.experimental.pallas import tpu as pltpu
from jax.sharding import PartitionSpec as P

GROUPS = 8
EXP_G = 2
LANES = 128
TILE = 8
MIB = 1 << 20
VMEM_LIMIT = 48 * MIB
RING = 4
DOWN_RING = 4
DOWN_CHUNKS = 2
SMALL_COST = pl.CostEstimate(flops=1, bytes_accessed=1, transcendentals=0)
STEP_COST = pl.CostEstimate(flops=1 << 29, bytes_accessed=1, transcendentals=0)
bf16 = jnp.bfloat16
f32 = jnp.float32


def swap(block, bits, count):
    return lax.ppermute(block, "wide", [(i, i ^ bits) for i in range(count)])


def half_roll(block):
    return pltpu.roll(block, TILE // 2, 0)


def low_half(shape):
    return lax.broadcasted_iota(jnp.int32, shape, 0) < TILE // 2


def unpack_pair(u, v):
    full = (u.shape[0] - TILE) // 2
    u_rest, v_rest = u[2 * full :], v[2 * full :]
    low = low_half(u_rest.shape)
    a = [u[:full], v[:full], jnp.where(low, u_rest, half_roll(v_rest))]
    b = [u[full : 2 * full], v[full : 2 * full], jnp.where(low, half_roll(u_rest), v_rest)]
    return a, b


def pack_pair(a, b):
    full = (a.shape[0] - TILE) // 2
    a_rest, b_rest = a[2 * full :], b[2 * full :]
    low = low_half(a_rest.shape)
    u = [a[:full], b[:full], jnp.where(low, a_rest, half_roll(b_rest))]
    v = [a[full : 2 * full], b[full : 2 * full], jnp.where(low, half_roll(a_rest), b_rest)]
    return u, v


def pack_columns(rows_ref, a, b):
    full = rows_ref.shape[0] - TILE
    a_rest, b_rest = rows_ref[full:, a], rows_ref[full:, b]
    rest = jnp.where(low_half(a_rest.shape), a_rest, half_roll(b_rest))
    return jnp.concatenate([rows_ref[:full, a], rows_ref[:full, b], rest], 0).astype(bf16)


def prepare_kernel(tokens_ref, ids_ref, gates_ref, whole_ref, first_ref, second_ref, rows_ref):
    rows, width = tokens_ref.shape
    half, cut = width // 2, first_ref.shape[1]
    rows_ref[0:rows, :width] = tokens_ref[...].astype(f32)
    experts = GROUPS * EXP_G
    catalog = lax.broadcasted_iota(jnp.int32, (experts, rows), 0)
    weight = jnp.zeros((experts, rows), f32)
    for k in range(ids_ref.shape[0]):
        weight = weight + jnp.where(ids_ref[k : k + 1, :] == catalog, gates_ref[k : k + 1, :], 0.0)
    row = lax.broadcasted_iota(jnp.int32, (experts, LANES), 0)
    eye = (row == lax.broadcasted_iota(jnp.int32, (experts, LANES), 1)).astype(bf16)
    rows_ref[0:rows, width : width + LANES] = lax.dot_general(
        weight.astype(bf16), eye, (((0,), (0,)), ((), ())), preferred_element_type=f32
    )
    rows_ref[:, width + LANES :] = jnp.zeros((rows_ref.shape[0], LANES), f32)
    first = pack_columns(rows_ref, slice(0, cut), slice(half, half + cut))
    second = pack_columns(rows_ref, slice(cut, half), slice(half + cut, width))
    route = pack_columns(rows_ref, slice(width, width + LANES), slice(width + LANES, width + 2 * LANES))
    first_ref[...] = first
    second_ref[:, : half - cut] = second
    second_ref[:, half - cut :] = route
    whole_ref[:, :cut] = first
    whole_ref[:, cut:half] = second
    whole_ref[:, half:] = route


def prepare(tokens, expert_ids, gates, cut):
    rows, width = tokens.shape
    half = width // 2
    padded = -(-rows // TILE) * TILE
    return pl.pallas_call(
        prepare_kernel,
        out_shape=[
            jax.ShapeDtypeStruct((2 * rows, half + LANES), bf16),
            jax.ShapeDtypeStruct((2 * rows, cut), bf16),
            jax.ShapeDtypeStruct((2 * rows, half - cut + LANES), bf16),
        ],
        scratch_shapes=[pltpu.VMEM((padded, width + 2 * LANES), f32)],
    )(tokens, expert_ids.T, gates.T)


def unpack_kernel(unit, places, size, refs, out_ref):
    def read(place, at, width):
        ref, number = refs[place[0]], place[1]
        return ref[number * unit : (number + 1) * unit, at : at + width].astype(f32)

    at = 0
    for first in range(0, len(places), 4):
        pieces_a, pieces_b, pieces_r = [], [], []
        for i in (first, first + 2):
            pair = places[i : i + 2]
            a, b = unpack_pair(*(read(p, p[2], size) for p in pair))
            pieces_a += a
            pieces_b += b
            if pair[0][3] is not None:
                pieces_r += unpack_pair(*(read(p, p[3], LANES) for p in pair))[0]
        rows_a = jnp.concatenate(pieces_a, 0)
        rows = slice(at, at + rows_a.shape[0])
        out_ref[rows, :size] = rows_a.astype(bf16)
        out_ref[rows, size : 2 * size] = jnp.concatenate(pieces_b, 0).astype(bf16)
        if pieces_r:
            out_ref[rows, 2 * size :] = jnp.concatenate(pieces_r, 0).astype(bf16)
        at = rows.stop


def unpack(arrays, unit, places, size):
    width = 2 * size + (0 if places[0][3] is None else LANES)

    def kernel(*refs):
        unpack_kernel(unit, places, size, refs[:-1], refs[-1])

    return call_small(kernel, jax.ShapeDtypeStruct((len(places) * unit // 2, width), bf16), arrays)


def stack(arrays):
    def kernel(*refs):
        at = 0
        for ref in refs[:-1]:
            refs[-1][at : at + ref.shape[0], :] = ref[...]
            at += ref.shape[0]

    rows = sum(a.shape[0] for a in arrays)
    return call_small(kernel, jax.ShapeDtypeStruct((rows, arrays[0].shape[1]), bf16), arrays)


def expert_kernel(unit, far, start, size, first, last, *refs):
    refs = list(refs)
    mine_ref, other_ref = refs[:2]
    refs = refs[2:]
    group_ref = refs.pop(0) if last else None
    prior_ref = None if first else refs.pop(0)
    gate_ref, up_ref = refs[:2]
    refs = refs[2:]
    if last:
        down_ref, keep_far_ref, send_far_ref, keep_ref, send_ref = refs[:5]
        refs = refs[5:]
    else:
        acc_ref = refs.pop(0)
    lhs_ref, ring_ref, sems = refs[:3]
    half = gate_ref.shape[1] // 2
    steps = [(expert, which) for expert in range(EXP_G) for which in range(2)]
    slots = ring_ref.shape[0]

    def fetch(step):
        expert, which = steps[step]
        source = (gate_ref, up_ref)[which]
        return [
            pltpu.make_async_copy(
                source.at[expert, pl.ds(side * half + start, size), :],
                ring_ref.at[step % slots, pl.ds(side * size, size), :],
                sems.at[step % slots, side],
            )
            for side in range(2)
        ]

    for step in range(slots):
        for copy in fetch(step):
            copy.start()
    if last:
        hidden_ref, down_ring_ref, down_sems = refs[3:6]
        down_slots, column = down_ring_ref.shape[0], down_ring_ref.shape[2] // 2
        down_steps = [(chunk, expert) for chunk in range(half // column) for expert in range(EXP_G)]

        def fetch_down(step):
            chunk, expert = down_steps[step]
            return [
                pltpu.make_async_copy(
                    down_ref.at[expert, :, pl.ds(side * half + chunk * column, column)],
                    down_ring_ref.at[step % down_slots, :, pl.ds(side * column, column)],
                    down_sems.at[step % down_slots, side],
                )
                for side in range(2)
            ]

        for step in range(down_slots):
            for copy in fetch_down(step):
                copy.start()
    rows = mine_ref.shape[0]
    lhs_ref[:rows, :] = mine_ref[:, : 2 * size]
    lhs_ref[rows:, :] = other_ref[:, : 2 * size]
    depth = gate_ref.shape[2]
    parts = []
    for step, (expert, which) in enumerate(steps):
        for copy in fetch(step):
            copy.wait()
        value = jnp.dot(lhs_ref[...], ring_ref[step % slots], preferred_element_type=f32)
        if step + slots < len(steps):
            for copy in fetch(step + slots):
                copy.start()
        if not first:
            value = value + prior_ref[expert, which]
        if not last:
            acc_ref[expert, which] = value
            continue
        parts.append(value)
        if which == 1:
            gate_value, lifted = parts[-2:]
            value = gate_value / (1.0 + jnp.exp(-gate_value)) * lifted
            for at, ref in ((0, mine_ref), (rows, other_ref)):
                route = ref[:, 2 * size :].astype(f32)
                lane = lax.broadcasted_iota(jnp.int32, route.shape, 1)
                scale = jnp.sum(jnp.where(lane == group_ref[0] * EXP_G + expert, route, 0.0), 1, keepdims=True)
                hidden_ref[expert, at : at + rows, :] = (value[at : at + rows] * scale).astype(bf16)
    if not last:
        return
    places = []
    for far_ref, ref in ((keep_far_ref, keep_ref), (send_far_ref, send_ref)):
        for near in range(2):
            places += [(ref, near * (far - 1) + far - 2 - f) for f in range(far - 1)] + [(far_ref, near)]
    total = None
    for step, (chunk, expert) in enumerate(down_steps):
        for copy in fetch_down(step):
            copy.wait()
        part = jnp.dot(hidden_ref[expert], down_ring_ref[step % down_slots], preferred_element_type=f32)
        if step + down_slots < len(down_steps):
            for copy in fetch_down(step + down_slots):
                copy.start()
        if expert == 0:
            total = part
            continue
        total = total + part
        if expert < EXP_G - 1:
            continue
        columns = slice(chunk * column, (chunk + 1) * column)
        for pair in range(len(places) // 2):
            block = total[pair * unit : (pair + 1) * unit]
            packed = pack_pair(block[:, :column], block[:, column:])
            for (ref, place), pieces in zip(places[2 * pair : 2 * pair + 2], packed, strict=True):
                ref[place * unit : (place + 1) * unit, columns] = jnp.concatenate(pieces, 0).astype(bf16)


def expert_step(mine, other, unit, start, size, group, prior, w_gate, w_up, w_down):
    first, last = prior is None, group is not None
    rows = 2 * mine.shape[0]
    far = rows // unit // 2
    depth = w_gate.shape[2]
    vmem = pl.BlockSpec(memory_space=pltpu.VMEM)
    hbm = pl.BlockSpec(memory_space=pl.ANY)
    smem = pl.BlockSpec(memory_space=pltpu.SMEM)
    scratch = [
        pltpu.VMEM((rows, 2 * size), bf16),
        pltpu.VMEM((RING, 2 * size, depth), bf16),
        pltpu.SemaphoreType.DMA((RING, 2)),
    ]
    args = [mine, other, *([group] if last else []), *([] if first else [prior]), w_gate, w_up]
    specs = [vmem] * 2 + [smem] * last + [vmem] * (not first) + [hbm, hbm]
    if last:
        args.append(w_down)
        specs.append(hbm)
        half = w_down.shape[2] // 2
        column = half // DOWN_CHUNKS
        few, many = (2 * unit, half), (2 * (far - 1) * unit, half)
        shapes = [jax.ShapeDtypeStruct(shape, bf16) for shape in (few, few, many, many)]
        scratch += [
            pltpu.VMEM((EXP_G, rows, depth), bf16),
            pltpu.VMEM((DOWN_RING, depth, 2 * column), bf16),
            pltpu.SemaphoreType.DMA((DOWN_RING, 2)),
        ]
    else:
        shapes = [jax.ShapeDtypeStruct((EXP_G, 2, rows, depth), f32)]
    return pl.pallas_call(
        functools.partial(expert_kernel, unit, far, start, size, first, last),
        out_shape=shapes,
        in_specs=specs,
        out_specs=[vmem] * len(shapes),
        scratch_shapes=scratch,
        compiler_params=pltpu.CompilerParams(vmem_limit_bytes=VMEM_LIMIT),
        cost_estimate=STEP_COST,
    )(*args)


def call_small(kernel, shapes, args, scratch=(), after=()):
    vmem = pl.BlockSpec(memory_space=pltpu.VMEM)

    def body(*refs):
        kernel(*refs[: len(args)], *refs[len(args) + len(after) :])

    return pl.pallas_call(
        body,
        out_shape=shapes,
        in_specs=[vmem] * len(args) + [pl.BlockSpec(memory_space=pl.ANY)] * len(after),
        out_specs=jax.tree.map(lambda _: vmem, shapes),
        scratch_shapes=list(scratch),
        compiler_params=pltpu.CompilerParams(vmem_limit_bytes=VMEM_LIMIT),
        cost_estimate=SMALL_COST,
    )(*args, *after)


def add_far(keep, got, cut):
    def kernel(keep_ref, got_ref, mine_ref, first_ref, second_ref):
        unit = mine_ref.shape[0]
        total = keep_ref[...].astype(f32) + got_ref[...].astype(f32)
        mine_ref[...] = total[:unit].astype(bf16)
        first_ref[...] = total[unit:, :cut].astype(bf16)
        second_ref[...] = total[unit:, cut:].astype(bf16)

    unit, half = keep.shape[0] // 2, keep.shape[1]
    shapes = [jax.ShapeDtypeStruct((unit, size), bf16) for size in (half, cut, half - cut)]
    return call_small(kernel, shapes, (keep, got))


def add_rest(keep, got, unit, after):
    few = keep.shape[0] // (2 * unit)

    def kernel(keep_ref, got_ref, mine_ref, *near_refs):
        total = keep_ref[...].astype(f32) + got_ref[...].astype(f32)
        mine_ref[...] = total[: few * unit].astype(bf16)
        for i, ref in enumerate(near_refs):
            ref[...] = total[(few + i) * unit : (few + i + 1) * unit].astype(bf16)

    shapes = [jax.ShapeDtypeStruct((rows, keep.shape[1]), bf16) for rows in [few * unit] + [unit] * few]
    mine, *nears = call_small(kernel, shapes, (keep, got), after=after)
    return mine, nears


def add_one(keep, number, columns, got):
    unit = got.shape[0]

    def kernel(keep_ref, got_ref, out_ref):
        kept = keep_ref[number * unit : (number + 1) * unit, columns]
        out_ref[...] = (kept.astype(f32) + got_ref[...].astype(f32)).astype(bf16)

    return call_small(kernel, jax.ShapeDtypeStruct(got.shape, bf16), (keep, got))


def finish(keep, got, wholes, first, second, rows):
    unit, half = got.shape
    cut = first.shape[1]
    padded = -(-rows // TILE) * TILE
    full = rows // TILE * TILE

    def kernel(keep_ref, *refs):
        first_ref, second_ref, out_ref, rows_ref = refs[-4:]
        for columns, part_ref in ((slice(0, cut), first_ref), (slice(cut, half), second_ref)):
            total = keep_ref[keep_ref.shape[0] - unit :, columns].astype(f32) + part_ref[...].astype(f32)
            for ref in refs[:-4]:
                total = total + ref[:, columns].astype(f32)
            a, b = columns, slice(half + columns.start, half + columns.stop)
            rest = total[2 * full :]
            rows_ref[:full, a] = total[:full]
            rows_ref[:full, b] = total[full : 2 * full]
            rows_ref[full:, a] = rest
            rows_ref[full:, b] = half_roll(rest)
        out_ref[...] = rows_ref[0:rows, :].astype(bf16)

    return call_small(
        kernel,
        jax.ShapeDtypeStruct((rows, 2 * half), bf16),
        (keep, got, *wholes, first, second),
        [pltpu.VMEM((padded, 2 * half), f32)],
    )


def local(tokens, expert_ids, gates, w_gate, w_up, w_down):
    count = lax.axis_size("wide")
    group_size = count // GROUPS
    far = count // 4
    rows, width = tokens.shape
    unit, half = 2 * rows, width // 2
    cut = half // 2 // (2 * LANES) * (2 * LANES)
    group = (lax.axis_index("wide") // group_size).astype(jnp.int32).reshape(1)

    whole, first, second = prepare(tokens, expert_ids, gates, cut)
    wholes = [whole] + [swap(whole, 4 * f, count) for f in range(1, far - 1)]
    first = swap(first, 4 * (far - 1), count)
    second = swap(second, 4 * (far - 1), count)
    nexts = [swap(stack(wholes[:2]), 2, count)] + [swap(block, 2, count) for block in wholes[2:]]
    first_next = swap(first, 2, count)
    second_next = swap(second, 2, count)

    def rows_of(last, last_next, start, size, routes):
        arrays = [*wholes, last, *nexts, last_next]
        places = [(i, 0) for i in range(far)] + [(far, 0), (far, 1)] + [(i, 0) for i in range(far + 1, len(arrays))]
        places = [(*p, *((0, size) if arrays[p[0]].shape[1] < half else (start, half))) for p in places]
        return unpack(arrays, unit, [(*p[:3], p[3] if routes else None) for p in places], size)

    mine = rows_of(first, first_next, 0, cut, False)
    other = swap(mine, 1, count)
    state = expert_step(mine, other, unit, 0, cut, None, None, w_gate, w_up, None)[0]
    mine = rows_of(second, second_next, cut, half - cut, True)
    other = swap(mine, 1, count)
    keep_far, send_far, keep, send = expert_step(
        mine, other, unit, cut, half - cut, group, state, w_gate, w_up, w_down
    )

    mine, *nears = add_far(keep_far, swap(send_far, 1, count), cut)
    last_far = []
    for near, columns in zip(nears, (slice(0, cut), slice(cut, half)), strict=True):
        got = swap(near, 2, count)
        last_far.append(swap(add_one(mine, 0, columns, got), 4 * (far - 1), count))
        if len(last_far) == 1:
            after = got
    mine, nears = add_rest(keep, swap(send, 1, count), unit, [after])
    parts = []
    for i, near in enumerate(nears):
        got = swap(near, 2, count)
        if i < far - 2:
            parts.append(swap(add_one(mine, i, slice(0, half), got), 4 * (far - 2 - i), count))
    return finish(mine, got, parts, *last_far, rows)


def solution(mesh):
    return jax.shard_map(
        local,
        mesh=mesh,
        in_specs=(
            P(("parts", "wide"), None),
            P(("parts", "wide"), None),
            P(("parts", "wide"), None),
            P(None, None, "wide"),
            P(None, None, "wide"),
            P(None, "wide", None),
        ),
        out_specs=P(("parts", "wide"), None),
        check_vma=False,
    )
```

```python
import functools

import jax
import jax.numpy as jnp
from jax import lax
from jax.experimental import pallas as pl
from jax.experimental.pallas import tpu as pltpu
from jax.sharding import PartitionSpec as P

GROUPS = 8
EXP_G = 2
LANES = 128
TILE = 8
MIB = 1 << 20
DOWN_CHUNKS = 4
SMALL_VMEM = 8 * MIB
PREPARE_VMEM = 58 * MIB
FIRST_VMEM = 36 * MIB
STEP_VMEM = 14 * MIB
DOWN_RING = 4
SMALL_COST = pl.CostEstimate(flops=1, bytes_accessed=1, transcendentals=0)
LOAD_COST = pl.CostEstimate(flops=1, bytes_accessed=1 << 24, transcendentals=0)
STEP_COST = pl.CostEstimate(flops=1 << 29, bytes_accessed=1, transcendentals=0)
bf16 = jnp.bfloat16
f32 = jnp.float32


def swap(block, bits, count):
    return lax.ppermute(block, "wide", [(i, i ^ bits) for i in range(count)])


def half_roll(block):
    return pltpu.roll(block, TILE // 2, 0)


def low_half(shape):
    return lax.broadcasted_iota(jnp.int32, shape, 0) < TILE // 2


def unpack_pair(u, v):
    full = (u.shape[0] - TILE) // 2
    u_rest, v_rest = u[2 * full :], v[2 * full :]
    low = low_half(u_rest.shape)
    a = [u[:full], v[:full], jnp.where(low, u_rest, half_roll(v_rest))]
    b = [u[full : 2 * full], v[full : 2 * full], jnp.where(low, half_roll(u_rest), v_rest)]
    return a, b


def pack_pair(a, b):
    full = (a.shape[0] - TILE) // 2
    a_rest, b_rest = a[2 * full :], b[2 * full :]
    low = low_half(a_rest.shape)
    u = [a[:full], b[:full], jnp.where(low, a_rest, half_roll(b_rest))]
    v = [a[full : 2 * full], b[full : 2 * full], jnp.where(low, half_roll(a_rest), b_rest)]
    return u, v


def pack_columns(rows_ref, a, b):
    full = rows_ref.shape[0] - TILE
    a_rest, b_rest = rows_ref[full:, a], rows_ref[full:, b]
    rest = jnp.where(low_half(a_rest.shape), a_rest, half_roll(b_rest))
    return jnp.concatenate([rows_ref[:full, a], rows_ref[:full, b], rest], 0).astype(bf16)


def prepare_kernel(tokens_hbm, ids_hbm, gates_hbm, out_ref, rows_ref, tokens_ref, ids_ref, gates_ref, sems):
    copies = [
        pltpu.make_async_copy(source, target, sems.at[i])
        for i, (source, target) in enumerate(
            ((tokens_hbm, tokens_ref), (ids_hbm, ids_ref), (gates_hbm, gates_ref))
        )
    ]
    for copy in copies:
        copy.start()
    for copy in copies:
        copy.wait()
    rows, width = tokens_ref.shape
    half = width // 2
    rows_ref[0:rows, :width] = tokens_ref[...].astype(f32)
    experts = GROUPS * EXP_G
    catalog = lax.broadcasted_iota(jnp.int32, (experts, rows), 0)
    weight = jnp.zeros((experts, rows), f32)
    for k in range(ids_ref.shape[0]):
        weight = weight + jnp.where(ids_ref[k : k + 1, :] == catalog, gates_ref[k : k + 1, :], 0.0)
    row = lax.broadcasted_iota(jnp.int32, (experts, LANES), 0)
    eye = (row == lax.broadcasted_iota(jnp.int32, (experts, LANES), 1)).astype(bf16)
    rows_ref[0:rows, width : width + LANES] = lax.dot_general(
        weight.astype(bf16), eye, (((0,), (0,)), ((), ())), preferred_element_type=f32
    )
    rows_ref[:, width + LANES :] = jnp.zeros((rows_ref.shape[0], LANES), f32)
    out_ref[:, :half] = pack_columns(rows_ref, slice(0, half), slice(half, width))
    out_ref[:, half:] = pack_columns(rows_ref, slice(width, width + LANES), slice(width + LANES, width + 2 * LANES))


def prepare(tokens, expert_ids, gates):
    rows, width = tokens.shape
    padded = -(-rows // TILE) * TILE
    args = (tokens, expert_ids.T, gates.T)
    return call_small(
        prepare_kernel,
        jax.ShapeDtypeStruct((2 * rows, width // 2 + LANES), bf16),
        (),
        [pltpu.VMEM((padded, width + 2 * LANES), f32)]
        + [pltpu.VMEM(a.shape, a.dtype) for a in args]
        + [pltpu.SemaphoreType.DMA((len(args),))],
        hbm=args,
        vmem_limit=PREPARE_VMEM,
    )


def preload(weights, vmem_limit):
    pieces = 4

    def kernel(source_ref, out_ref, sems):
        rows = weights.shape[1] // pieces
        copies = [
            pltpu.make_async_copy(
                source_ref.at[e, pl.ds(i * rows, rows), :], out_ref.at[e, pl.ds(i * rows, rows), :], sems.at[e, i]
            )
            for e in range(EXP_G)
            for i in range(pieces)
        ]
        for copy in copies:
            copy.start()
        for copy in copies:
            copy.wait()

    return call_small(
        kernel,
        jax.ShapeDtypeStruct(weights.shape, weights.dtype),
        (),
        [pltpu.SemaphoreType.DMA((EXP_G, pieces))],
        hbm=(weights,),
        cost=LOAD_COST,
        vmem_limit=vmem_limit,
    )


def unpack(blocks, unit):
    arrays = [array for array, _ in blocks]
    half = arrays[0].shape[1] - LANES

    def kernel(*refs):
        out_ref = refs[-1]
        values = [
            ref[number * unit : (number + 1) * unit, :].astype(f32)
            for ref, (_, number) in zip(refs[:-1], blocks, strict=True)
        ]
        pieces = []
        for i in (0, 2):
            a, b = unpack_pair(*values[i : i + 2])
            pieces.append((jnp.concatenate(a, 0), jnp.concatenate(b, 0)))
        rows_a, rows_b = (jnp.concatenate(part, 0) for part in zip(*pieces, strict=True))
        out_ref[:, :half] = rows_a[:, :half].astype(bf16)
        out_ref[:, half : 2 * half] = rows_b[:, :half].astype(bf16)
        out_ref[:, 2 * half :] = rows_a[:, half:].astype(bf16)

    shape = jax.ShapeDtypeStruct((len(blocks) * unit // 2, 2 * half + LANES), bf16)
    return call_small(kernel, shape, arrays)


def stack(arrays, *after):
    def kernel(*refs):
        at = 0
        for ref in refs[:-1]:
            refs[-1][at : at + ref.shape[0], :] = ref[...]
            at += ref.shape[0]

    rows = sum(a.shape[0] for a in arrays)
    return call_small(kernel, jax.ShapeDtypeStruct((rows, arrays[0].shape[1]), bf16), arrays, after=after)


def hold(block, *after, cost=None):
    return call_small(
        lambda block_ref, out_ref: out_ref.__setitem__(..., block_ref[...]),
        jax.ShapeDtypeStruct(block.shape, block.dtype),
        (block,),
        after=after,
        cost=cost or SMALL_COST,
    )


def expert_kernel(unit, far, count, *refs):
    blocks, refs = refs[:count], refs[count:]
    gate_ref, up_ref, down_ref, keep_far_ref, send_far_ref, keep_ref, send_ref = refs[:7]
    lhs_ref, hidden_ref, ring_ref, sems = refs[7:]
    width, depth = gate_ref.shape[1:]
    half = width // 2
    slots, column = ring_ref.shape[0], ring_ref.shape[2] // 2
    steps = [(chunk, expert) for chunk in range(half // column) for expert in range(EXP_G)]

    def fetch(step):
        chunk, expert = steps[step]
        return [
            pltpu.make_async_copy(
                down_ref.at[expert, :, pl.ds(side * half + chunk * column, column)],
                ring_ref.at[step % slots, :, pl.ds(side * column, column)],
                sems.at[step % slots, side],
            )
            for side in range(2)
        ]

    for step in range(slots):
        for copy in fetch(step):
            copy.start()
    at = 0
    scales = []
    group = lax.axis_index("wide") // (lax.axis_size("wide") // GROUPS)
    for ref in blocks:
        rows = slice(at, at + ref.shape[0])
        lhs_ref[rows, :] = ref[:, :width]
        route = ref[:, width:].astype(f32)
        lane = lax.broadcasted_iota(jnp.int32, route.shape, 1)
        scales.append(
            [
                jnp.sum(jnp.where(lane == group * EXP_G + expert, route, 0.0), 1, keepdims=True)
                for expert in range(EXP_G)
            ]
        )
        at = rows.stop
    for expert in range(EXP_G):
        gate_value = jnp.dot(lhs_ref[...], gate_ref[expert], preferred_element_type=f32)
        lifted = jnp.dot(lhs_ref[...], up_ref[expert], preferred_element_type=f32)
        value = gate_value / (1.0 + jnp.exp(-gate_value)) * lifted
        scale = jnp.concatenate([pair[expert] for pair in scales], 0)
        hidden_ref[expert] = (value * scale).astype(bf16)
    places = []
    for far_ref, ref in ((keep_far_ref, keep_ref), (send_far_ref, send_ref)):
        for first in range(0, far, 2):
            for near in range(2):
                for f in (first, first + 1):
                    places.append((far_ref, near) if f == far - 1 else (ref, near * (far - 1) + far - 2 - f))
    total = None
    for step, (chunk, expert) in enumerate(steps):
        for copy in fetch(step):
            copy.wait()
        part = jnp.dot(hidden_ref[expert], ring_ref[step % slots], preferred_element_type=f32)
        if step + slots < len(steps):
            for copy in fetch(step + slots):
                copy.start()
        if expert == 0:
            total = part
            continue
        total = total + part
        if expert < EXP_G - 1:
            continue
        columns = slice(chunk * column, (chunk + 1) * column)
        for pair in range(len(places) // 2):
            block = total[pair * unit : (pair + 1) * unit]
            packed = pack_pair(block[:, :column], block[:, column:])
            for (ref, place), parts in zip(places[2 * pair : 2 * pair + 2], packed, strict=True):
                ref[place * unit : (place + 1) * unit, columns] = jnp.concatenate(parts, 0).astype(bf16)


def expert_step(blocks, unit, w_gate, w_up, w_down):
    rows = sum(b.shape[0] for b in blocks)
    far = rows // unit // 2
    _, width, depth = w_up.shape
    half = width // 2
    column = half // DOWN_CHUNKS
    vmem = pl.BlockSpec(memory_space=pltpu.VMEM)
    few, many = (2 * unit, half), (2 * (far - 1) * unit, half)
    return pl.pallas_call(
        functools.partial(expert_kernel, unit, far, len(blocks)),
        out_shape=[jax.ShapeDtypeStruct(shape, bf16) for shape in (few, few, many, many)],
        in_specs=[vmem] * (len(blocks) + 2) + [pl.BlockSpec(memory_space=pl.ANY)],
        out_specs=[vmem] * 4,
        scratch_shapes=[
            pltpu.VMEM((rows, width), bf16),
            pltpu.VMEM((EXP_G, rows, depth), bf16),
            pltpu.VMEM((DOWN_RING, depth, 2 * column), bf16),
            pltpu.SemaphoreType.DMA((DOWN_RING, 2)),
        ],
        compiler_params=pltpu.CompilerParams(vmem_limit_bytes=STEP_VMEM),
        cost_estimate=STEP_COST,
    )(*blocks, w_gate, w_up, w_down)


def call_small(kernel, shapes, args, scratch=(), after=(), hbm=(), cost=SMALL_COST, vmem_limit=SMALL_VMEM):
    vmem = pl.BlockSpec(memory_space=pltpu.VMEM)
    count = len(args) + len(hbm)

    def body(*refs):
        kernel(*refs[:count], *refs[count + len(after) :])

    return pl.pallas_call(
        body,
        out_shape=shapes,
        in_specs=[vmem] * len(args) + [pl.BlockSpec(memory_space=pl.ANY)] * (len(hbm) + len(after)),
        out_specs=jax.tree.map(lambda _: vmem, shapes),
        scratch_shapes=list(scratch),
        compiler_params=pltpu.CompilerParams(vmem_limit_bytes=vmem_limit),
        cost_estimate=cost,
    )(*args, *hbm, *after)


def add_far(keep, got):
    unit = keep.shape[0] // 2

    def kernel(keep_ref, got_ref, mine_ref, near_ref):
        total = keep_ref[...].astype(f32) + got_ref[...].astype(f32)
        mine_ref[...] = total[:unit].astype(bf16)
        near_ref[...] = total[unit:].astype(bf16)

    return call_small(kernel, [jax.ShapeDtypeStruct((unit, keep.shape[1]), bf16)] * 2, (keep, got))


def add_rest(keep, got, unit, after):
    few = keep.shape[0] // (2 * unit)

    def kernel(keep_ref, got_ref, mine_ref, *near_refs):
        total = keep_ref[...].astype(f32) + got_ref[...].astype(f32)
        mine_ref[...] = total[: few * unit].astype(bf16)
        for i, ref in enumerate(near_refs):
            ref[...] = total[(few + i) * unit : (few + i + 1) * unit].astype(bf16)

    shapes = [jax.ShapeDtypeStruct((rows, keep.shape[1]), bf16) for rows in [few * unit] + [unit] * few]
    mine, *nears = call_small(kernel, shapes, (keep, got), after=after)
    return mine, nears


def add_one(keep, number, got, after=()):
    unit = got.shape[0]

    def kernel(keep_ref, got_ref, out_ref):
        kept = keep_ref[number * unit : (number + 1) * unit, :]
        out_ref[...] = (kept.astype(f32) + got_ref[...].astype(f32)).astype(bf16)

    return call_small(kernel, jax.ShapeDtypeStruct(got.shape, bf16), (keep, got), after=after)


def finish(keep, got, parts, rows):
    unit, half = got.shape
    padded = -(-rows // TILE) * TILE
    full = rows // TILE * TILE

    def kernel(keep_ref, *refs):
        out_ref, rows_ref = refs[-2:]
        total = keep_ref[keep_ref.shape[0] - unit :, :].astype(f32)
        for ref in refs[:-2]:
            total = total + ref[...].astype(f32)
        rest = total[2 * full :]
        rows_ref[:full, :half] = total[:full]
        rows_ref[:full, half:] = total[full : 2 * full]
        rows_ref[full:, :half] = rest
        rows_ref[full:, half:] = half_roll(rest)
        out_ref[...] = rows_ref[0:rows, :].astype(bf16)

    return call_small(
        kernel,
        jax.ShapeDtypeStruct((rows, 2 * half), bf16),
        (keep, got, *parts),
        [pltpu.VMEM((padded, 2 * half), f32)],
    )


def local(tokens, expert_ids, gates, w_gate, w_up, w_down):
    count = lax.axis_size("wide")
    far = count // 4
    rows, width = tokens.shape
    unit, half = 2 * rows, width // 2

    whole = prepare(tokens, expert_ids, gates)
    blocks = [whole] + [swap(whole, 4 * f, count) for f in range(1, far)]
    gate, up = w_gate, preload(w_up, FIRST_VMEM)
    pair = swap(stack(blocks[:2], up), 2, count)
    nexts = [(pair, 0), (pair, 1)] + [(swap(block, 2, count), 0) for block in blocks[2:]]
    blocks = [(block, 0) for block in blocks]
    mine = [unpack(blocks[f : f + 2] + nexts[f : f + 2], unit) for f in range(0, far, 2)]
    other = [swap(rows_of, 1, count) for rows_of in mine]
    keep_far, send_far, keep, send = expert_step(mine + other, unit, gate, up, w_down)

    got = swap(send_far, 1, count)
    mine, near = add_far(keep_far, got)
    send = hold(send, got)
    got = swap(near, 2, count)
    last_far = hold(swap(add_one(mine, 0, got), 4 * (far - 1), count), cost=LOAD_COST)
    mine, nears = add_rest(keep, swap(send, 1, count), unit, [got])
    parts = [last_far]
    for i, near in enumerate(nears):
        got = swap(near, 2, count)
        if i < far - 2:
            parts.append(swap(add_one(mine, i, got), 4 * (far - 2 - i), count))
    return finish(mine, got, parts, rows)


def solution(mesh):
    return jax.shard_map(
        local,
        mesh=mesh,
        in_specs=(
            P(("parts", "wide"), None),
            P(("parts", "wide"), None),
            P(("parts", "wide"), None),
            P(None, None, "wide"),
            P(None, None, "wide"),
            P(None, "wide", None),
        ),
        out_specs=P(("parts", "wide"), None),
        check_vma=False,
    )
```

```python
import functools

import jax
import jax.numpy as jnp
from jax import lax
from jax.experimental import pallas as pl
from jax.experimental.pallas import tpu as pltpu
from jax.sharding import PartitionSpec as P

GROUPS = 8
EXP_G = 2
LANES = 128
TILE = 8
MIB = 1 << 20
DOWN_CHUNKS = 4
SMALL_VMEM = 8 * MIB
PREPARE_VMEM = 58 * MIB
FIRST_VMEM = 36 * MIB
STEP_VMEM = 14 * MIB
DOWN_RING = 4
SMALL_COST = pl.CostEstimate(flops=1, bytes_accessed=1, transcendentals=0)
LOAD_COST = pl.CostEstimate(flops=1, bytes_accessed=1 << 24, transcendentals=0)
STEP_COST = pl.CostEstimate(flops=1 << 29, bytes_accessed=1, transcendentals=0)
bf16 = jnp.bfloat16
f32 = jnp.float32


def swap(block, bits, count):
    return lax.ppermute(block, "wide", [(i, i ^ bits) for i in range(count)])


def half_roll(block):
    return pltpu.roll(block, TILE // 2, 0)


def low_half(shape):
    return lax.broadcasted_iota(jnp.int32, shape, 0) < TILE // 2


def unpack_pair(u, v):
    full = (u.shape[0] - TILE) // 2
    u_rest, v_rest = u[2 * full :], v[2 * full :]
    low = low_half(u_rest.shape)
    a = [u[:full], v[:full], jnp.where(low, u_rest, half_roll(v_rest))]
    b = [u[full : 2 * full], v[full : 2 * full], jnp.where(low, half_roll(u_rest), v_rest)]
    return a, b


def pack_pair(a, b):
    full = (a.shape[0] - TILE) // 2
    a_rest, b_rest = a[2 * full :], b[2 * full :]
    low = low_half(a_rest.shape)
    u = [a[:full], b[:full], jnp.where(low, a_rest, half_roll(b_rest))]
    v = [a[full : 2 * full], b[full : 2 * full], jnp.where(low, half_roll(a_rest), b_rest)]
    return u, v


def pack_columns(rows_ref, a, b):
    full = rows_ref.shape[0] - TILE
    a_rest, b_rest = rows_ref[full:, a], rows_ref[full:, b]
    rest = jnp.where(low_half(a_rest.shape), a_rest, half_roll(b_rest))
    return jnp.concatenate([rows_ref[:full, a], rows_ref[:full, b], rest], 0).astype(bf16)


def prepare_kernel(tokens_hbm, ids_hbm, gates_hbm, out_ref, rows_ref, tokens_ref, ids_ref, gates_ref, sems):
    copies = [
        pltpu.make_async_copy(source, target, sems.at[i])
        for i, (source, target) in enumerate(
            ((tokens_hbm, tokens_ref), (ids_hbm, ids_ref), (gates_hbm, gates_ref))
        )
    ]
    for copy in copies:
        copy.start()
    for copy in copies:
        copy.wait()
    rows, width = tokens_ref.shape
    half = width // 2
    rows_ref[0:rows, :width] = tokens_ref[...].astype(f32)
    experts = GROUPS * EXP_G
    catalog = lax.broadcasted_iota(jnp.int32, (experts, rows), 0)
    weight = jnp.zeros((experts, rows), f32)
    for k in range(ids_ref.shape[0]):
        weight = weight + jnp.where(ids_ref[k : k + 1, :] == catalog, gates_ref[k : k + 1, :], 0.0)
    row = lax.broadcasted_iota(jnp.int32, (experts, LANES), 0)
    eye = (row == lax.broadcasted_iota(jnp.int32, (experts, LANES), 1)).astype(bf16)
    rows_ref[0:rows, width : width + LANES] = lax.dot_general(
        weight.astype(bf16), eye, (((0,), (0,)), ((), ())), preferred_element_type=f32
    )
    rows_ref[:, width + LANES :] = jnp.zeros((rows_ref.shape[0], LANES), f32)
    out_ref[:, :half] = pack_columns(rows_ref, slice(0, half), slice(half, width))
    out_ref[:, half:] = pack_columns(rows_ref, slice(width, width + LANES), slice(width + LANES, width + 2 * LANES))


def prepare(tokens, expert_ids, gates):
    rows, width = tokens.shape
    padded = -(-rows // TILE) * TILE
    args = (tokens, expert_ids.T, gates.T)
    return call_small(
        prepare_kernel,
        jax.ShapeDtypeStruct((2 * rows, width // 2 + LANES), bf16),
        (),
        [pltpu.VMEM((padded, width + 2 * LANES), f32)]
        + [pltpu.VMEM(a.shape, a.dtype) for a in args]
        + [pltpu.SemaphoreType.DMA((len(args),))],
        hbm=args,
        vmem_limit=PREPARE_VMEM,
    )


def preload(weights, vmem_limit):
    pieces = 4

    def kernel(source_ref, out_ref, sems):
        rows = weights.shape[1] // pieces
        copies = [
            pltpu.make_async_copy(
                source_ref.at[e, pl.ds(i * rows, rows), :], out_ref.at[e, pl.ds(i * rows, rows), :], sems.at[e, i]
            )
            for e in range(EXP_G)
            for i in range(pieces)
        ]
        for copy in copies:
            copy.start()
        for copy in copies:
            copy.wait()

    return call_small(
        kernel,
        jax.ShapeDtypeStruct(weights.shape, weights.dtype),
        (),
        [pltpu.SemaphoreType.DMA((EXP_G, pieces))],
        hbm=(weights,),
        cost=LOAD_COST,
        vmem_limit=vmem_limit,
    )


def unpack(blocks, unit):
    arrays = [array for array, _ in blocks]
    half = arrays[0].shape[1] - LANES

    def kernel(*refs):
        out_ref = refs[-1]
        values = [
            ref[number * unit : (number + 1) * unit, :].astype(f32)
            for ref, (_, number) in zip(refs[:-1], blocks, strict=True)
        ]
        pieces = []
        for i in (0, 2):
            a, b = unpack_pair(*values[i : i + 2])
            pieces.append((jnp.concatenate(a, 0), jnp.concatenate(b, 0)))
        rows_a, rows_b = (jnp.concatenate(part, 0) for part in zip(*pieces, strict=True))
        out_ref[:, :half] = rows_a[:, :half].astype(bf16)
        out_ref[:, half : 2 * half] = rows_b[:, :half].astype(bf16)
        out_ref[:, 2 * half :] = rows_a[:, half:].astype(bf16)

    shape = jax.ShapeDtypeStruct((len(blocks) * unit // 2, 2 * half + LANES), bf16)
    return call_small(kernel, shape, arrays)


def stack(arrays, *after):
    def kernel(*refs):
        at = 0
        for ref in refs[:-1]:
            refs[-1][at : at + ref.shape[0], :] = ref[...]
            at += ref.shape[0]

    rows = sum(a.shape[0] for a in arrays)
    return call_small(kernel, jax.ShapeDtypeStruct((rows, arrays[0].shape[1]), bf16), arrays, after=after)


def hold(block, *after, cost=None):
    return call_small(
        lambda block_ref, out_ref: out_ref.__setitem__(..., block_ref[...]),
        jax.ShapeDtypeStruct(block.shape, block.dtype),
        (block,),
        after=after,
        cost=cost or SMALL_COST,
    )


def expert_kernel(unit, far, count, *refs):
    blocks, refs = refs[:count], refs[count:]
    gate_ref, up_ref, down_ref, keep_far_ref, send_far_ref, keep_ref, send_ref = refs[:7]
    lhs_ref, hidden_ref, ring_ref, sems = refs[7:]
    width, depth = gate_ref.shape[1:]
    half = width // 2
    slots, column = ring_ref.shape[0], ring_ref.shape[2] // 2
    steps = [(chunk, expert) for chunk in range(half // column) for expert in range(EXP_G)]

    def fetch(step):
        chunk, expert = steps[step]
        return [
            pltpu.make_async_copy(
                down_ref.at[expert, :, pl.ds(side * half + chunk * column, column)],
                ring_ref.at[step % slots, :, pl.ds(side * column, column)],
                sems.at[step % slots, side],
            )
            for side in range(2)
        ]

    for step in range(slots):
        for copy in fetch(step):
            copy.start()
    at = 0
    scales = []
    group = lax.axis_index("wide") // (lax.axis_size("wide") // GROUPS)
    for ref in blocks:
        rows = slice(at, at + ref.shape[0])
        lhs_ref[rows, :] = ref[:, :width]
        route = ref[:, width:].astype(f32)
        lane = lax.broadcasted_iota(jnp.int32, route.shape, 1)
        scales.append(
            [
                jnp.sum(jnp.where(lane == group * EXP_G + expert, route, 0.0), 1, keepdims=True)
                for expert in range(EXP_G)
            ]
        )
        at = rows.stop
    for expert in range(EXP_G):
        gate_value = jnp.dot(lhs_ref[...], gate_ref[expert], preferred_element_type=f32)
        lifted = jnp.dot(lhs_ref[...], up_ref[expert], preferred_element_type=f32)
        value = gate_value / (1.0 + jnp.exp(-gate_value)) * lifted
        scale = jnp.concatenate([pair[expert] for pair in scales], 0)
        hidden_ref[expert] = (value * scale).astype(bf16)
    places = []
    for far_ref, ref in ((keep_far_ref, keep_ref), (send_far_ref, send_ref)):
        for first in range(0, far, 2):
            for near in range(2):
                for f in (first, first + 1):
                    places.append((far_ref, near) if f == far - 1 else (ref, near * (far - 1) + far - 2 - f))
    total = None
    for step, (chunk, expert) in enumerate(steps):
        for copy in fetch(step):
            copy.wait()
        part = jnp.dot(hidden_ref[expert], ring_ref[step % slots], preferred_element_type=f32)
        if step + slots < len(steps):
            for copy in fetch(step + slots):
                copy.start()
        if expert == 0:
            total = part
            continue
        total = total + part
        if expert < EXP_G - 1:
            continue
        columns = slice(chunk * column, (chunk + 1) * column)
        for pair in range(len(places) // 2):
            block = total[pair * unit : (pair + 1) * unit]
            packed = pack_pair(block[:, :column], block[:, column:])
            for (ref, place), parts in zip(places[2 * pair : 2 * pair + 2], packed, strict=True):
                ref[place * unit : (place + 1) * unit, columns] = jnp.concatenate(parts, 0).astype(bf16)


def expert_step(blocks, unit, w_gate, w_up, w_down):
    rows = sum(b.shape[0] for b in blocks)
    far = rows // unit // 2
    _, width, depth = w_up.shape
    half = width // 2
    column = half // DOWN_CHUNKS
    vmem = pl.BlockSpec(memory_space=pltpu.VMEM)
    few, many = (2 * unit, half), (2 * (far - 1) * unit, half)
    return pl.pallas_call(
        functools.partial(expert_kernel, unit, far, len(blocks)),
        out_shape=[jax.ShapeDtypeStruct(shape, bf16) for shape in (few, few, many, many)],
        in_specs=[vmem] * (len(blocks) + 2) + [pl.BlockSpec(memory_space=pl.ANY)],
        out_specs=[vmem] * 4,
        scratch_shapes=[
            pltpu.VMEM((rows, width), bf16),
            pltpu.VMEM((EXP_G, rows, depth), bf16),
            pltpu.VMEM((DOWN_RING, depth, 2 * column), bf16),
            pltpu.SemaphoreType.DMA((DOWN_RING, 2)),
        ],
        compiler_params=pltpu.CompilerParams(vmem_limit_bytes=STEP_VMEM),
        cost_estimate=STEP_COST,
    )(*blocks, w_gate, w_up, w_down)


def call_small(kernel, shapes, args, scratch=(), after=(), hbm=(), cost=SMALL_COST, vmem_limit=SMALL_VMEM):
    vmem = pl.BlockSpec(memory_space=pltpu.VMEM)
    count = len(args) + len(hbm)

    def body(*refs):
        kernel(*refs[:count], *refs[count + len(after) :])

    return pl.pallas_call(
        body,
        out_shape=shapes,
        in_specs=[vmem] * len(args) + [pl.BlockSpec(memory_space=pl.ANY)] * (len(hbm) + len(after)),
        out_specs=jax.tree.map(lambda _: vmem, shapes),
        scratch_shapes=list(scratch),
        compiler_params=pltpu.CompilerParams(vmem_limit_bytes=vmem_limit),
        cost_estimate=cost,
    )(*args, *hbm, *after)


def add_far(keep, got):
    unit = keep.shape[0] // 2

    def kernel(keep_ref, got_ref, mine_ref, near_ref):
        total = keep_ref[...].astype(f32) + got_ref[...].astype(f32)
        mine_ref[...] = total[:unit].astype(bf16)
        near_ref[...] = total[unit:].astype(bf16)

    return call_small(kernel, [jax.ShapeDtypeStruct((unit, keep.shape[1]), bf16)] * 2, (keep, got))


def add_rest(keep, got, unit, after):
    few = keep.shape[0] // (2 * unit)

    def kernel(keep_ref, got_ref, mine_ref, *near_refs):
        total = keep_ref[...].astype(f32) + got_ref[...].astype(f32)
        mine_ref[...] = total[: few * unit].astype(bf16)
        for i, ref in enumerate(near_refs):
            ref[...] = total[(few + i) * unit : (few + i + 1) * unit].astype(bf16)

    shapes = [jax.ShapeDtypeStruct((rows, keep.shape[1]), bf16) for rows in [few * unit] + [unit] * few]
    mine, *nears = call_small(kernel, shapes, (keep, got), after=after)
    return mine, nears


def add_one(keep, number, got, after=()):
    unit = got.shape[0]

    def kernel(keep_ref, got_ref, out_ref):
        kept = keep_ref[number * unit : (number + 1) * unit, :]
        out_ref[...] = (kept.astype(f32) + got_ref[...].astype(f32)).astype(bf16)

    return call_small(kernel, jax.ShapeDtypeStruct(got.shape, bf16), (keep, got), after=after)


def finish(keep, got, parts, rows):
    unit, half = got.shape
    padded = -(-rows // TILE) * TILE
    full = rows // TILE * TILE

    def kernel(keep_ref, *refs):
        out_ref, rows_ref = refs[-2:]
        total = keep_ref[keep_ref.shape[0] - unit :, :].astype(f32)
        for ref in refs[:-2]:
            total = total + ref[...].astype(f32)
        rest = total[2 * full :]
        rows_ref[:full, :half] = total[:full]
        rows_ref[:full, half:] = total[full : 2 * full]
        rows_ref[full:, :half] = rest
        rows_ref[full:, half:] = half_roll(rest)
        out_ref[...] = rows_ref[0:rows, :].astype(bf16)

    return call_small(
        kernel,
        jax.ShapeDtypeStruct((rows, 2 * half), bf16),
        (keep, got, *parts),
        [pltpu.VMEM((padded, 2 * half), f32)],
    )


def local(tokens, expert_ids, gates, w_gate, w_up, w_down):
    count = lax.axis_size("wide")
    far = count // 4
    rows, width = tokens.shape
    unit, half = 2 * rows, width // 2

    whole = prepare(tokens, expert_ids, gates)
    blocks = [whole] + [swap(whole, 4 * f, count) for f in range(1, far)]
    gate, up = w_gate, preload(w_up, FIRST_VMEM)
    pair = swap(stack(blocks[:2], up), 2, count)
    nexts = [(pair, 0), (pair, 1)] + [(swap(block, 2, count), 0) for block in blocks[2:]]
    blocks = [(block, 0) for block in blocks]
    mine = [unpack(blocks[f : f + 2] + nexts[f : f + 2], unit) for f in range(0, far, 2)]
    other = [swap(rows_of, 1, count) for rows_of in mine]
    keep_far, send_far, keep, send = expert_step(mine + other, unit, gate, up, w_down)

    got = swap(send_far, 1, count)
    mine, near = add_far(keep_far, got)
    send = hold(send, got)
    got = swap(near, 2, count)
    last_far = hold(swap(add_one(mine, 0, got), 4 * (far - 1), count), cost=LOAD_COST)
    mine, nears = add_rest(keep, swap(send, 1, count), unit, [])
    parts = [last_far]
    for i, near in enumerate(nears):
        got = swap(near, 2, count)
        if i < far - 2:
            parts.append(swap(add_one(mine, i, got), 4 * (far - 2 - i), count))
    return finish(mine, got, parts, rows)


def solution(mesh):
    return jax.shard_map(
        local,
        mesh=mesh,
        in_specs=(
            P(("parts", "wide"), None),
            P(("parts", "wide"), None),
            P(("parts", "wide"), None),
            P(None, None, "wide"),
            P(None, None, "wide"),
            P(None, "wide", None),
        ),
        out_specs=P(("parts", "wide"), None),
        check_vma=False,
    )
```

```python
import functools

import jax
import jax.numpy as jnp
from jax import lax
from jax.experimental import pallas as pl
from jax.experimental.pallas import tpu as pltpu
from jax.sharding import PartitionSpec as P

GROUPS = 8
EXP_G = 2
LANES = 128
TILE = 8
MIB = 1 << 20
GATE_CHUNKS = 2
DOWN_CHUNKS = 4
SMALL_VMEM = 8 * MIB
PREPARE_VMEM = 58 * MIB
FIRST_VMEM = 36 * MIB
STEP_VMEM = 15 * MIB
DOWN_RING = 4
SMALL_COST = pl.CostEstimate(flops=1, bytes_accessed=1, transcendentals=0)
LOAD_COST = pl.CostEstimate(flops=1, bytes_accessed=1 << 24, transcendentals=0)
STEP_COST = pl.CostEstimate(flops=1 << 29, bytes_accessed=1, transcendentals=0)
bf16 = jnp.bfloat16
f32 = jnp.float32


def swap(block, bits, count):
    return lax.ppermute(block, "wide", [(i, i ^ bits) for i in range(count)])


def half_roll(block):
    return pltpu.roll(block, TILE // 2, 0)


def low_half(shape):
    return lax.broadcasted_iota(jnp.int32, shape, 0) < TILE // 2


def unpack_pair(u, v):
    full = (u.shape[0] - TILE) // 2
    u_rest, v_rest = u[2 * full :], v[2 * full :]
    low = low_half(u_rest.shape)
    a = [u[:full], v[:full], jnp.where(low, u_rest, half_roll(v_rest))]
    b = [u[full : 2 * full], v[full : 2 * full], jnp.where(low, half_roll(u_rest), v_rest)]
    return a, b


def pack_pair(a, b):
    full = (a.shape[0] - TILE) // 2
    a_rest, b_rest = a[2 * full :], b[2 * full :]
    low = low_half(a_rest.shape)
    u = [a[:full], b[:full], jnp.where(low, a_rest, half_roll(b_rest))]
    v = [a[full : 2 * full], b[full : 2 * full], jnp.where(low, half_roll(a_rest), b_rest)]
    return u, v


def pack_columns(rows_ref, a, b):
    full = rows_ref.shape[0] - TILE
    a_rest, b_rest = rows_ref[full:, a], rows_ref[full:, b]
    rest = jnp.where(low_half(a_rest.shape), a_rest, half_roll(b_rest))
    return jnp.concatenate([rows_ref[:full, a], rows_ref[:full, b], rest], 0).astype(bf16)


def prepare_kernel(tokens_hbm, ids_hbm, gates_hbm, out_ref, rows_ref, tokens_ref, ids_ref, gates_ref, sems):
    copies = [
        pltpu.make_async_copy(source, target, sems.at[i])
        for i, (source, target) in enumerate(
            ((tokens_hbm, tokens_ref), (ids_hbm, ids_ref), (gates_hbm, gates_ref))
        )
    ]
    for copy in copies:
        copy.start()
    for copy in copies:
        copy.wait()
    rows, width = tokens_ref.shape
    half = width // 2
    rows_ref[0:rows, :width] = tokens_ref[...].astype(f32)
    experts = GROUPS * EXP_G
    catalog = lax.broadcasted_iota(jnp.int32, (experts, rows), 0)
    weight = jnp.zeros((experts, rows), f32)
    for k in range(ids_ref.shape[0]):
        weight = weight + jnp.where(ids_ref[k : k + 1, :] == catalog, gates_ref[k : k + 1, :], 0.0)
    row = lax.broadcasted_iota(jnp.int32, (experts, LANES), 0)
    eye = (row == lax.broadcasted_iota(jnp.int32, (experts, LANES), 1)).astype(bf16)
    rows_ref[0:rows, width : width + LANES] = lax.dot_general(
        weight.astype(bf16), eye, (((0,), (0,)), ((), ())), preferred_element_type=f32
    )
    rows_ref[:, width + LANES :] = jnp.zeros((rows_ref.shape[0], LANES), f32)
    out_ref[:, :half] = pack_columns(rows_ref, slice(0, half), slice(half, width))
    out_ref[:, half:] = pack_columns(rows_ref, slice(width, width + LANES), slice(width + LANES, width + 2 * LANES))


def prepare(tokens, expert_ids, gates):
    rows, width = tokens.shape
    padded = -(-rows // TILE) * TILE
    args = (tokens, expert_ids.T, gates.T)
    return call_small(
        prepare_kernel,
        jax.ShapeDtypeStruct((2 * rows, width // 2 + LANES), bf16),
        (),
        [pltpu.VMEM((padded, width + 2 * LANES), f32)]
        + [pltpu.VMEM(a.shape, a.dtype) for a in args]
        + [pltpu.SemaphoreType.DMA((len(args),))],
        hbm=args,
        vmem_limit=PREPARE_VMEM,
    )


def preload(weights, vmem_limit):
    pieces = 4

    def kernel(source_ref, out_ref, sems):
        rows = weights.shape[1] // pieces
        copies = [
            pltpu.make_async_copy(
                source_ref.at[e, pl.ds(i * rows, rows), :], out_ref.at[e, pl.ds(i * rows, rows), :], sems.at[e, i]
            )
            for e in range(EXP_G)
            for i in range(pieces)
        ]
        for copy in copies:
            copy.start()
        for copy in copies:
            copy.wait()

    return call_small(
        kernel,
        jax.ShapeDtypeStruct(weights.shape, weights.dtype),
        (),
        [pltpu.SemaphoreType.DMA((EXP_G, pieces))],
        hbm=(weights,),
        cost=LOAD_COST,
        vmem_limit=vmem_limit,
    )


def unpack(blocks, unit):
    arrays = [array for array, _ in blocks]
    half = arrays[0].shape[1] - LANES

    def kernel(*refs):
        out_ref = refs[-1]
        values = [
            ref[number * unit : (number + 1) * unit, :].astype(f32)
            for ref, (_, number) in zip(refs[:-1], blocks, strict=True)
        ]
        pieces = []
        for i in (0, 2):
            a, b = unpack_pair(*values[i : i + 2])
            pieces.append((jnp.concatenate(a, 0), jnp.concatenate(b, 0)))
        rows_a, rows_b = (jnp.concatenate(part, 0) for part in zip(*pieces, strict=True))
        out_ref[:, :half] = rows_a[:, :half].astype(bf16)
        out_ref[:, half : 2 * half] = rows_b[:, :half].astype(bf16)
        out_ref[:, 2 * half :] = rows_a[:, half:].astype(bf16)

    shape = jax.ShapeDtypeStruct((len(blocks) * unit // 2, 2 * half + LANES), bf16)
    return call_small(kernel, shape, arrays)


def stack(arrays, *after):
    def kernel(*refs):
        at = 0
        for ref in refs[:-1]:
            refs[-1][at : at + ref.shape[0], :] = ref[...]
            at += ref.shape[0]

    rows = sum(a.shape[0] for a in arrays)
    return call_small(kernel, jax.ShapeDtypeStruct((rows, arrays[0].shape[1]), bf16), arrays, after=after)


def hold(block, *after, cost=None):
    return call_small(
        lambda block_ref, out_ref: out_ref.__setitem__(..., block_ref[...]),
        jax.ShapeDtypeStruct(block.shape, block.dtype),
        (block,),
        after=after,
        cost=cost or SMALL_COST,
    )


def expert_kernel(unit, far, count, *refs):
    blocks, refs = refs[:count], refs[count:]
    gate_ref, up_ref, down_ref, keep_far_ref, send_far_ref, keep_ref, send_ref = refs[:7]
    lhs_ref, hidden_ref, ring_ref, sems = refs[7:]
    width, depth = gate_ref.shape[1:]
    half = width // 2
    slots, column = ring_ref.shape[0], ring_ref.shape[2] // 2
    steps = [(chunk, expert) for chunk in range(half // column) for expert in range(EXP_G)]

    def fetch(step):
        chunk, expert = steps[step]
        return [
            pltpu.make_async_copy(
                down_ref.at[expert, :, pl.ds(side * half + chunk * column, column)],
                ring_ref.at[step % slots, :, pl.ds(side * column, column)],
                sems.at[step % slots, side],
            )
            for side in range(2)
        ]

    for step in range(slots):
        for copy in fetch(step):
            copy.start()
    group = lax.axis_index("wide") // (lax.axis_size("wide") // GROUPS)
    at = 0
    for ref in blocks:
        lhs_ref[at : at + ref.shape[0], :] = ref[:, :width]
        at += ref.shape[0]
    part = depth // GATE_CHUNKS

    def hidden_part(i, carry):
        expert = i // GATE_CHUNKS
        columns = pl.ds(pl.multiple_of(i % GATE_CHUNKS * part, part), part)
        gate_value = jnp.dot(lhs_ref[...], gate_ref[expert, :, columns], preferred_element_type=f32)
        lifted = jnp.dot(lhs_ref[...], up_ref[expert, :, columns], preferred_element_type=f32)
        scales = []
        for ref in blocks:
            route = ref[:, width:].astype(f32)
            lane = lax.broadcasted_iota(jnp.int32, route.shape, 1)
            scales.append(jnp.sum(jnp.where(lane == group * EXP_G + expert, route, 0.0), 1, keepdims=True))
        value = gate_value / (1.0 + jnp.exp(-gate_value)) * lifted * jnp.concatenate(scales, 0)
        hidden_ref[expert, :, columns] = value.astype(bf16)
        return carry

    lax.fori_loop(0, EXP_G * GATE_CHUNKS, hidden_part, 0)
    places = []
    for far_ref, ref in ((keep_far_ref, keep_ref), (send_far_ref, send_ref)):
        for first in range(0, far, 2):
            for near in range(2):
                for f in (first, first + 1):
                    places.append((far_ref, near) if f == far - 1 else (ref, near * (far - 1) + far - 2 - f))
    total = None
    for step, (chunk, expert) in enumerate(steps):
        for copy in fetch(step):
            copy.wait()
        part = jnp.dot(hidden_ref[expert], ring_ref[step % slots], preferred_element_type=f32)
        if step + slots < len(steps):
            for copy in fetch(step + slots):
                copy.start()
        if expert == 0:
            total = part
            continue
        total = total + part
        if expert < EXP_G - 1:
            continue
        columns = slice(chunk * column, (chunk + 1) * column)
        for pair in range(len(places) // 2):
            block = total[pair * unit : (pair + 1) * unit]
            packed = pack_pair(block[:, :column], block[:, column:])
            for (ref, place), parts in zip(places[2 * pair : 2 * pair + 2], packed, strict=True):
                ref[place * unit : (place + 1) * unit, columns] = jnp.concatenate(parts, 0).astype(bf16)


def expert_step(blocks, unit, w_gate, w_up, w_down):
    rows = sum(b.shape[0] for b in blocks)
    far = rows // unit // 2
    _, width, depth = w_up.shape
    half = width // 2
    column = half // DOWN_CHUNKS
    vmem = pl.BlockSpec(memory_space=pltpu.VMEM)
    few, many = (2 * unit, half), (2 * (far - 1) * unit, half)
    return pl.pallas_call(
        functools.partial(expert_kernel, unit, far, len(blocks)),
        out_shape=[jax.ShapeDtypeStruct(shape, bf16) for shape in (few, few, many, many)],
        in_specs=[vmem] * (len(blocks) + 2) + [pl.BlockSpec(memory_space=pl.ANY)],
        out_specs=[vmem] * 4,
        scratch_shapes=[
            pltpu.VMEM((rows, width), bf16),
            pltpu.VMEM((EXP_G, rows, depth), bf16),
            pltpu.VMEM((DOWN_RING, depth, 2 * column), bf16),
            pltpu.SemaphoreType.DMA((DOWN_RING, 2)),
        ],
        compiler_params=pltpu.CompilerParams(vmem_limit_bytes=STEP_VMEM),
        cost_estimate=STEP_COST,
    )(*blocks, w_gate, w_up, w_down)


def call_small(kernel, shapes, args, scratch=(), after=(), hbm=(), cost=SMALL_COST, vmem_limit=SMALL_VMEM):
    vmem = pl.BlockSpec(memory_space=pltpu.VMEM)
    count = len(args) + len(hbm)

    def body(*refs):
        kernel(*refs[:count], *refs[count + len(after) :])

    return pl.pallas_call(
        body,
        out_shape=shapes,
        in_specs=[vmem] * len(args) + [pl.BlockSpec(memory_space=pl.ANY)] * (len(hbm) + len(after)),
        out_specs=jax.tree.map(lambda _: vmem, shapes),
        scratch_shapes=list(scratch),
        compiler_params=pltpu.CompilerParams(vmem_limit_bytes=vmem_limit),
        cost_estimate=cost,
    )(*args, *hbm, *after)


def add_far(keep, got):
    unit = keep.shape[0] // 2

    def kernel(keep_ref, got_ref, mine_ref, near_ref):
        total = keep_ref[...].astype(f32) + got_ref[...].astype(f32)
        mine_ref[...] = total[:unit].astype(bf16)
        near_ref[...] = total[unit:].astype(bf16)

    return call_small(kernel, [jax.ShapeDtypeStruct((unit, keep.shape[1]), bf16)] * 2, (keep, got))


def add_rest(keep, got, unit, after):
    few = keep.shape[0] // (2 * unit)

    def kernel(keep_ref, got_ref, mine_ref, *near_refs):
        total = keep_ref[...].astype(f32) + got_ref[...].astype(f32)
        mine_ref[...] = total[: few * unit].astype(bf16)
        for i, ref in enumerate(near_refs):
            ref[...] = total[(few + i) * unit : (few + i + 1) * unit].astype(bf16)

    shapes = [jax.ShapeDtypeStruct((rows, keep.shape[1]), bf16) for rows in [few * unit] + [unit] * few]
    mine, *nears = call_small(kernel, shapes, (keep, got), after=after)
    return mine, nears


def add_one(keep, number, got, after=()):
    unit = got.shape[0]

    def kernel(keep_ref, got_ref, out_ref):
        kept = keep_ref[number * unit : (number + 1) * unit, :]
        out_ref[...] = (kept.astype(f32) + got_ref[...].astype(f32)).astype(bf16)

    return call_small(kernel, jax.ShapeDtypeStruct(got.shape, bf16), (keep, got), after=after)


def finish(keep, got, parts, rows):
    unit, half = got.shape
    padded = -(-rows // TILE) * TILE
    full = rows // TILE * TILE

    def kernel(keep_ref, *refs):
        out_ref, rows_ref = refs[-2:]
        total = keep_ref[keep_ref.shape[0] - unit :, :].astype(f32)
        for ref in refs[:-2]:
            total = total + ref[...].astype(f32)
        rest = total[2 * full :]
        rows_ref[:full, :half] = total[:full]
        rows_ref[:full, half:] = total[full : 2 * full]
        rows_ref[full:, :half] = rest
        rows_ref[full:, half:] = half_roll(rest)
        out_ref[...] = rows_ref[0:rows, :].astype(bf16)

    return call_small(
        kernel,
        jax.ShapeDtypeStruct((rows, 2 * half), bf16),
        (keep, got, *parts),
        [pltpu.VMEM((padded, 2 * half), f32)],
    )


def local(tokens, expert_ids, gates, w_gate, w_up, w_down):
    count = lax.axis_size("wide")
    far = count // 4
    rows, width = tokens.shape
    unit, half = 2 * rows, width // 2

    whole = prepare(tokens, expert_ids, gates)
    blocks = [whole] + [swap(whole, 4 * f, count) for f in range(1, far)]
    gate, up = w_gate, preload(w_up, FIRST_VMEM)
    pair = swap(stack(blocks[:2], up), 2, count)
    nexts = [(pair, 0), (pair, 1)] + [(swap(block, 2, count), 0) for block in blocks[2:]]
    blocks = [(block, 0) for block in blocks]
    mine = [unpack(blocks[f : f + 2] + nexts[f : f + 2], unit) for f in range(0, far, 2)]
    other = [swap(rows_of, 1, count) for rows_of in mine]
    keep_far, send_far, keep, send = expert_step(mine + other, unit, gate, up, w_down)

    got = swap(send_far, 1, count)
    mine, near = add_far(keep_far, got)
    send = hold(send, got)
    got = swap(near, 2, count)
    last_far = hold(swap(add_one(mine, 0, got), 4 * (far - 1), count), cost=LOAD_COST)
    mine, nears = add_rest(keep, swap(send, 1, count), unit, [])
    parts = [last_far]
    for i, near in enumerate(nears):
        got = swap(near, 2, count)
        if i < far - 2:
            parts.append(swap(add_one(mine, i, got), 4 * (far - 2 - i), count))
    return finish(mine, got, parts, rows)


def solution(mesh):
    return jax.shard_map(
        local,
        mesh=mesh,
        in_specs=(
            P(("parts", "wide"), None),
            P(("parts", "wide"), None),
            P(("parts", "wide"), None),
            P(None, None, "wide"),
            P(None, None, "wide"),
            P(None, "wide", None),
        ),
        out_specs=P(("parts", "wide"), None),
        check_vma=False,
    )
```

```python
import functools

import jax
import jax.numpy as jnp
from jax import lax
from jax.experimental import pallas as pl
from jax.experimental.pallas import tpu as pltpu
from jax.sharding import PartitionSpec as P

GROUPS = 8
EXP_G = 2
LANES = 128
TILE = 8
MIB = 1 << 20
GATE_CHUNKS = 2
DOWN_CHUNKS = 4
SMALL_VMEM = 8 * MIB
PREPARE_VMEM = 58 * MIB
FIRST_VMEM = 30 * MIB
STEP_VMEM = 15 * MIB
DOWN_RING = 4
SMALL_COST = pl.CostEstimate(flops=1, bytes_accessed=1, transcendentals=0)
LOAD_COST = pl.CostEstimate(flops=1, bytes_accessed=1 << 24, transcendentals=0)
STEP_COST = pl.CostEstimate(flops=1 << 29, bytes_accessed=1, transcendentals=0)
bf16 = jnp.bfloat16
f32 = jnp.float32


def swap(block, bits, count):
    return lax.ppermute(block, "wide", [(i, i ^ bits) for i in range(count)])


def half_roll(block):
    return pltpu.roll(block, TILE // 2, 0)


def low_half(shape):
    return lax.broadcasted_iota(jnp.int32, shape, 0) < TILE // 2


def unpack_pair(u, v):
    full = (u.shape[0] - TILE) // 2
    u_rest, v_rest = u[2 * full :], v[2 * full :]
    low = low_half(u_rest.shape)
    a = [u[:full], v[:full], jnp.where(low, u_rest, half_roll(v_rest))]
    b = [u[full : 2 * full], v[full : 2 * full], jnp.where(low, half_roll(u_rest), v_rest)]
    return a, b


def pack_pair(a, b):
    full = (a.shape[0] - TILE) // 2
    a_rest, b_rest = a[2 * full :], b[2 * full :]
    low = low_half(a_rest.shape)
    u = [a[:full], b[:full], jnp.where(low, a_rest, half_roll(b_rest))]
    v = [a[full : 2 * full], b[full : 2 * full], jnp.where(low, half_roll(a_rest), b_rest)]
    return u, v


def pack_columns(rows_ref, a, b):
    full = rows_ref.shape[0] - TILE
    a_rest, b_rest = rows_ref[full:, a], rows_ref[full:, b]
    rest = jnp.where(low_half(a_rest.shape), a_rest, half_roll(b_rest))
    return jnp.concatenate([rows_ref[:full, a], rows_ref[:full, b], rest], 0).astype(bf16)


def prepare_kernel(tokens_hbm, ids_hbm, gates_hbm, out_ref, rows_ref, tokens_ref, ids_ref, gates_ref, sems):
    copies = [
        pltpu.make_async_copy(source, target, sems.at[i])
        for i, (source, target) in enumerate(
            ((tokens_hbm, tokens_ref), (ids_hbm, ids_ref), (gates_hbm, gates_ref))
        )
    ]
    for copy in copies:
        copy.start()
    for copy in copies:
        copy.wait()
    rows, width = tokens_ref.shape
    half = width // 2
    rows_ref[0:rows, :width] = tokens_ref[...].astype(f32)
    experts = GROUPS * EXP_G
    catalog = lax.broadcasted_iota(jnp.int32, (experts, rows), 0)
    weight = jnp.zeros((experts, rows), f32)
    for k in range(ids_ref.shape[0]):
        weight = weight + jnp.where(ids_ref[k : k + 1, :] == catalog, gates_ref[k : k + 1, :], 0.0)
    row = lax.broadcasted_iota(jnp.int32, (experts, LANES), 0)
    eye = (row == lax.broadcasted_iota(jnp.int32, (experts, LANES), 1)).astype(bf16)
    rows_ref[0:rows, width : width + LANES] = lax.dot_general(
        weight.astype(bf16), eye, (((0,), (0,)), ((), ())), preferred_element_type=f32
    )
    rows_ref[:, width + LANES :] = jnp.zeros((rows_ref.shape[0], LANES), f32)
    out_ref[:, :half] = pack_columns(rows_ref, slice(0, half), slice(half, width))
    out_ref[:, half:] = pack_columns(rows_ref, slice(width, width + LANES), slice(width + LANES, width + 2 * LANES))


def prepare(tokens, expert_ids, gates):
    rows, width = tokens.shape
    padded = -(-rows // TILE) * TILE
    args = (tokens, expert_ids.T, gates.T)
    return call_small(
        prepare_kernel,
        jax.ShapeDtypeStruct((2 * rows, width // 2 + LANES), bf16),
        (),
        [pltpu.VMEM((padded, width + 2 * LANES), f32)]
        + [pltpu.VMEM(a.shape, a.dtype) for a in args]
        + [pltpu.SemaphoreType.DMA((len(args),))],
        hbm=args,
        vmem_limit=PREPARE_VMEM,
    )


def preload(weights, vmem_limit):
    pieces = 4

    def kernel(source_ref, out_ref, sems):
        rows = weights.shape[1] // pieces
        copies = [
            pltpu.make_async_copy(
                source_ref.at[e, pl.ds(i * rows, rows), :], out_ref.at[e, pl.ds(i * rows, rows), :], sems.at[e, i]
            )
            for e in range(EXP_G)
            for i in range(pieces)
        ]
        for copy in copies:
            copy.start()
        for copy in copies:
            copy.wait()

    return call_small(
        kernel,
        jax.ShapeDtypeStruct(weights.shape, weights.dtype),
        (),
        [pltpu.SemaphoreType.DMA((EXP_G, pieces))],
        hbm=(weights,),
        cost=LOAD_COST,
        vmem_limit=vmem_limit,
    )


def unpack(blocks, unit):
    arrays = [array for array, _ in blocks]
    half = arrays[0].shape[1] - LANES

    def kernel(*refs):
        out_ref = refs[-1]
        values = [
            ref[number * unit : (number + 1) * unit, :].astype(f32)
            for ref, (_, number) in zip(refs[:-1], blocks, strict=True)
        ]
        pieces = []
        for i in (0, 2):
            a, b = unpack_pair(*values[i : i + 2])
            pieces.append((jnp.concatenate(a, 0), jnp.concatenate(b, 0)))
        rows_a, rows_b = (jnp.concatenate(part, 0) for part in zip(*pieces, strict=True))
        out_ref[:, :half] = rows_a[:, :half].astype(bf16)
        out_ref[:, half : 2 * half] = rows_b[:, :half].astype(bf16)
        out_ref[:, 2 * half :] = rows_a[:, half:].astype(bf16)

    shape = jax.ShapeDtypeStruct((len(blocks) * unit // 2, 2 * half + LANES), bf16)
    return call_small(kernel, shape, arrays)


def stack(arrays, *after):
    def kernel(*refs):
        at = 0
        for ref in refs[:-1]:
            refs[-1][at : at + ref.shape[0], :] = ref[...]
            at += ref.shape[0]

    rows = sum(a.shape[0] for a in arrays)
    return call_small(kernel, jax.ShapeDtypeStruct((rows, arrays[0].shape[1]), bf16), arrays, after=after)


def hold(block, *after, cost=None):
    return call_small(
        lambda block_ref, out_ref: out_ref.__setitem__(..., block_ref[...]),
        jax.ShapeDtypeStruct(block.shape, block.dtype),
        (block,),
        after=after,
        cost=cost or SMALL_COST,
    )


def expert_kernel(unit, far, count, *refs):
    blocks, refs = refs[:count], refs[count:]
    gate_ref, up_ref, down_ref, keep_far_ref, send_far_ref, keep_ref, send_ref = refs[:7]
    lhs_ref, hidden_ref, ring_ref, sems = refs[7:]
    width, depth = gate_ref.shape[1:]
    half = width // 2
    slots, column = ring_ref.shape[0], ring_ref.shape[2] // 2
    steps = [(chunk, expert) for chunk in range(half // column) for expert in range(EXP_G)]

    def fetch(step):
        chunk, expert = steps[step]
        return [
            pltpu.make_async_copy(
                down_ref.at[expert, :, pl.ds(side * half + chunk * column, column)],
                ring_ref.at[step % slots, :, pl.ds(side * column, column)],
                sems.at[step % slots, side],
            )
            for side in range(2)
        ]

    for step in range(slots):
        for copy in fetch(step):
            copy.start()
    group = lax.axis_index("wide") // (lax.axis_size("wide") // GROUPS)
    at = 0
    for ref in blocks:
        lhs_ref[at : at + ref.shape[0], :] = ref[:, :width]
        at += ref.shape[0]
    part = depth // GATE_CHUNKS

    def hidden_part(i, carry):
        expert = i // GATE_CHUNKS
        columns = pl.ds(pl.multiple_of(i % GATE_CHUNKS * part, part), part)
        gate_value = jnp.dot(lhs_ref[...], gate_ref[expert, :, columns], preferred_element_type=f32)
        lifted = jnp.dot(lhs_ref[...], up_ref[expert, :, columns], preferred_element_type=f32)
        scales = []
        for ref in blocks:
            route = ref[:, width:].astype(f32)
            lane = lax.broadcasted_iota(jnp.int32, route.shape, 1)
            scales.append(jnp.sum(jnp.where(lane == group * EXP_G + expert, route, 0.0), 1, keepdims=True))
        value = gate_value / (1.0 + jnp.exp(-gate_value)) * lifted * jnp.concatenate(scales, 0)
        hidden_ref[expert, :, columns] = value.astype(bf16)
        return carry

    lax.fori_loop(0, EXP_G * GATE_CHUNKS, hidden_part, 0)
    places = []
    for far_ref, ref in ((keep_far_ref, keep_ref), (send_far_ref, send_ref)):
        for first in range(0, far, 2):
            for near in range(2):
                for f in (first, first + 1):
                    places.append((far_ref, near) if f == far - 1 else (ref, near * (far - 1) + far - 2 - f))
    total = None
    for step, (chunk, expert) in enumerate(steps):
        for copy in fetch(step):
            copy.wait()
        part = jnp.dot(hidden_ref[expert], ring_ref[step % slots], preferred_element_type=f32)
        if step + slots < len(steps):
            for copy in fetch(step + slots):
                copy.start()
        if expert == 0:
            total = part
            continue
        total = total + part
        if expert < EXP_G - 1:
            continue
        columns = slice(chunk * column, (chunk + 1) * column)
        for pair in range(len(places) // 2):
            block = total[pair * unit : (pair + 1) * unit]
            packed = pack_pair(block[:, :column], block[:, column:])
            for (ref, place), parts in zip(places[2 * pair : 2 * pair + 2], packed, strict=True):
                ref[place * unit : (place + 1) * unit, columns] = jnp.concatenate(parts, 0).astype(bf16)


def expert_step(blocks, unit, w_gate, w_up, w_down):
    rows = sum(b.shape[0] for b in blocks)
    far = rows // unit // 2
    _, width, depth = w_up.shape
    half = width // 2
    column = half // DOWN_CHUNKS
    vmem = pl.BlockSpec(memory_space=pltpu.VMEM)
    few, many = (2 * unit, half), (2 * (far - 1) * unit, half)
    return pl.pallas_call(
        functools.partial(expert_kernel, unit, far, len(blocks)),
        out_shape=[jax.ShapeDtypeStruct(shape, bf16) for shape in (few, few, many, many)],
        in_specs=[vmem] * (len(blocks) + 2) + [pl.BlockSpec(memory_space=pl.ANY)],
        out_specs=[vmem] * 4,
        scratch_shapes=[
            pltpu.VMEM((rows, width), bf16),
            pltpu.VMEM((EXP_G, rows, depth), bf16),
            pltpu.VMEM((DOWN_RING, depth, 2 * column), bf16),
            pltpu.SemaphoreType.DMA((DOWN_RING, 2)),
        ],
        compiler_params=pltpu.CompilerParams(vmem_limit_bytes=STEP_VMEM),
        cost_estimate=STEP_COST,
    )(*blocks, w_gate, w_up, w_down)


def call_small(kernel, shapes, args, scratch=(), after=(), hbm=(), cost=SMALL_COST, vmem_limit=SMALL_VMEM):
    vmem = pl.BlockSpec(memory_space=pltpu.VMEM)
    count = len(args) + len(hbm)

    def body(*refs):
        kernel(*refs[:count], *refs[count + len(after) :])

    return pl.pallas_call(
        body,
        out_shape=shapes,
        in_specs=[vmem] * len(args) + [pl.BlockSpec(memory_space=pl.ANY)] * (len(hbm) + len(after)),
        out_specs=jax.tree.map(lambda _: vmem, shapes),
        scratch_shapes=list(scratch),
        compiler_params=pltpu.CompilerParams(vmem_limit_bytes=vmem_limit),
        cost_estimate=cost,
    )(*args, *hbm, *after)


def add_far(keep, got):
    unit = keep.shape[0] // 2

    def kernel(keep_ref, got_ref, mine_ref, near_ref):
        total = keep_ref[...].astype(f32) + got_ref[...].astype(f32)
        mine_ref[...] = total[:unit].astype(bf16)
        near_ref[...] = total[unit:].astype(bf16)

    return call_small(kernel, [jax.ShapeDtypeStruct((unit, keep.shape[1]), bf16)] * 2, (keep, got))


def add_rest(keep, got, unit, after):
    few = keep.shape[0] // (2 * unit)

    def kernel(keep_ref, got_ref, mine_ref, *near_refs):
        total = keep_ref[...].astype(f32) + got_ref[...].astype(f32)
        mine_ref[...] = total[: few * unit].astype(bf16)
        for i, ref in enumerate(near_refs):
            ref[...] = total[(few + i) * unit : (few + i + 1) * unit].astype(bf16)

    shapes = [jax.ShapeDtypeStruct((rows, keep.shape[1]), bf16) for rows in [few * unit] + [unit] * few]
    mine, *nears = call_small(kernel, shapes, (keep, got), after=after)
    return mine, nears


def add_one(keep, number, got, after=()):
    unit = got.shape[0]

    def kernel(keep_ref, got_ref, out_ref):
        kept = keep_ref[number * unit : (number + 1) * unit, :]
        out_ref[...] = (kept.astype(f32) + got_ref[...].astype(f32)).astype(bf16)

    return call_small(kernel, jax.ShapeDtypeStruct(got.shape, bf16), (keep, got), after=after)


def finish(keep, got, parts, rows):
    unit, half = got.shape
    padded = -(-rows // TILE) * TILE
    full = rows // TILE * TILE

    def kernel(keep_ref, *refs):
        out_ref, rows_ref = refs[-2:]
        total = keep_ref[keep_ref.shape[0] - unit :, :].astype(f32)
        for ref in refs[:-2]:
            total = total + ref[...].astype(f32)
        rest = total[2 * full :]
        rows_ref[:full, :half] = total[:full]
        rows_ref[:full, half:] = total[full : 2 * full]
        rows_ref[full:, :half] = rest
        rows_ref[full:, half:] = half_roll(rest)
        out_ref[...] = rows_ref[0:rows, :].astype(bf16)

    return call_small(
        kernel,
        jax.ShapeDtypeStruct((rows, 2 * half), bf16),
        (keep, got, *parts),
        [pltpu.VMEM((padded, 2 * half), f32)],
    )


def local(tokens, expert_ids, gates, w_gate, w_up, w_down):
    count = lax.axis_size("wide")
    far = count // 4
    rows, width = tokens.shape
    unit, half = 2 * rows, width // 2

    whole = prepare(tokens, expert_ids, gates)
    blocks = [whole] + [swap(whole, 4 * f, count) for f in range(1, far)]
    gate, up = w_gate, preload(w_up, FIRST_VMEM)
    pair = swap(stack(blocks[:2]), 2, count)
    nexts = [(pair, 0), (pair, 1)]
    nexts += [(swap(hold(block, up) if f == far - 2 else block, 2, count), 0) for f, block in enumerate(blocks) if f > 1]
    blocks = [(block, 0) for block in blocks]
    mine = [unpack(blocks[f : f + 2] + nexts[f : f + 2], unit) for f in range(0, far, 2)]
    other = [swap(rows_of, 1, count) for rows_of in mine]
    keep_far, send_far, keep, send = expert_step(mine + other, unit, gate, up, w_down)

    got = swap(send_far, 1, count)
    mine, near = add_far(keep_far, got)
    send = hold(send, got)
    got = swap(near, 2, count)
    last_far = hold(swap(add_one(mine, 0, got), 4 * (far - 1), count), cost=LOAD_COST)
    mine, nears = add_rest(keep, swap(send, 1, count), unit, [])
    parts = [last_far]
    for i, near in enumerate(nears):
        got = swap(near, 2, count)
        if i < far - 2:
            parts.append(swap(add_one(mine, i, got), 4 * (far - 2 - i), count))
    return finish(mine, got, parts, rows)


def solution(mesh):
    return jax.shard_map(
        local,
        mesh=mesh,
        in_specs=(
            P(("parts", "wide"), None),
            P(("parts", "wide"), None),
            P(("parts", "wide"), None),
            P(None, None, "wide"),
            P(None, None, "wide"),
            P(None, "wide", None),
        ),
        out_specs=P(("parts", "wide"), None),
        check_vma=False,
    )
```

```python
import functools

import jax
import jax.numpy as jnp
from jax import lax
from jax.experimental import pallas as pl
from jax.experimental.pallas import tpu as pltpu
from jax.sharding import PartitionSpec as P

GROUPS = 8
EXP_G = 2
LANES = 128
TILE = 8
MIB = 1 << 20
GATE_CHUNKS = 2
DOWN_CHUNKS = 4
SMALL_VMEM = 8 * MIB
PREPARE_VMEM = 58 * MIB
FIRST_VMEM = 30 * MIB
STEP_VMEM = 15 * MIB
DOWN_RING = 4
SMALL_COST = pl.CostEstimate(flops=1, bytes_accessed=1, transcendentals=0)
LOAD_COST = pl.CostEstimate(flops=1, bytes_accessed=1 << 24, transcendentals=0)
STEP_COST = pl.CostEstimate(flops=1 << 29, bytes_accessed=1, transcendentals=0)
bf16 = jnp.bfloat16
f32 = jnp.float32


def swap(block, bits, count):
    return lax.ppermute(block, "wide", [(i, i ^ bits) for i in range(count)])


def half_roll(block):
    return pltpu.roll(block, TILE // 2, 0)


def low_half(shape):
    return lax.broadcasted_iota(jnp.int32, shape, 0) < TILE // 2


def unpack_pair(u, v):
    full = (u.shape[0] - TILE) // 2
    u_rest, v_rest = u[2 * full :], v[2 * full :]
    low = low_half(u_rest.shape)
    a = [u[:full], v[:full], jnp.where(low, u_rest, half_roll(v_rest))]
    b = [u[full : 2 * full], v[full : 2 * full], jnp.where(low, half_roll(u_rest), v_rest)]
    return a, b


def pack_pair(a, b):
    full = (a.shape[0] - TILE) // 2
    a_rest, b_rest = a[2 * full :], b[2 * full :]
    low = low_half(a_rest.shape)
    u = [a[:full], b[:full], jnp.where(low, a_rest, half_roll(b_rest))]
    v = [a[full : 2 * full], b[full : 2 * full], jnp.where(low, half_roll(a_rest), b_rest)]
    return u, v


def pack_columns(rows_ref, a, b):
    full = rows_ref.shape[0] - TILE
    a_rest, b_rest = rows_ref[full:, a], rows_ref[full:, b]
    rest = jnp.where(low_half(a_rest.shape), a_rest, half_roll(b_rest))
    return jnp.concatenate([rows_ref[:full, a], rows_ref[:full, b], rest], 0).astype(bf16)


def prepare_kernel(tokens_hbm, ids_hbm, gates_hbm, out_ref, rows_ref, tokens_ref, ids_ref, gates_ref, sems):
    copies = [
        pltpu.make_async_copy(source, target, sems.at[i])
        for i, (source, target) in enumerate(
            ((tokens_hbm, tokens_ref), (ids_hbm, ids_ref), (gates_hbm, gates_ref))
        )
    ]
    for copy in copies:
        copy.start()
    for copy in copies[1:]:
        copy.wait()
    rows, width = tokens_ref.shape
    half = width // 2
    experts = GROUPS * EXP_G
    catalog = lax.broadcasted_iota(jnp.int32, (experts, rows), 0)
    weight = jnp.zeros((experts, rows), f32)
    for k in range(ids_ref.shape[0]):
        weight = weight + jnp.where(ids_ref[k : k + 1, :] == catalog, gates_ref[k : k + 1, :], 0.0)
    row = lax.broadcasted_iota(jnp.int32, (experts, LANES), 0)
    eye = (row == lax.broadcasted_iota(jnp.int32, (experts, LANES), 1)).astype(bf16)
    rows_ref[0:rows, width : width + LANES] = lax.dot_general(
        weight.astype(bf16), eye, (((0,), (0,)), ((), ())), preferred_element_type=f32
    )
    rows_ref[:, width + LANES :] = jnp.zeros((rows_ref.shape[0], LANES), f32)
    copies[0].wait()
    rows_ref[0:rows, :width] = tokens_ref[...].astype(f32)
    out_ref[:, :half] = pack_columns(rows_ref, slice(0, half), slice(half, width))
    out_ref[:, half:] = pack_columns(rows_ref, slice(width, width + LANES), slice(width + LANES, width + 2 * LANES))


def prepare(tokens, expert_ids, gates):
    rows, width = tokens.shape
    padded = -(-rows // TILE) * TILE
    args = (tokens, expert_ids.T, gates.T)
    return call_small(
        prepare_kernel,
        jax.ShapeDtypeStruct((2 * rows, width // 2 + LANES), bf16),
        (),
        [pltpu.VMEM((padded, width + 2 * LANES), f32)]
        + [pltpu.VMEM(a.shape, a.dtype) for a in args]
        + [pltpu.SemaphoreType.DMA((len(args),))],
        hbm=args,
        vmem_limit=PREPARE_VMEM,
    )


def preload(weights, vmem_limit):
    pieces = 4

    def kernel(source_ref, out_ref, sems):
        rows = weights.shape[1] // pieces
        copies = [
            pltpu.make_async_copy(
                source_ref.at[e, pl.ds(i * rows, rows), :], out_ref.at[e, pl.ds(i * rows, rows), :], sems.at[e, i]
            )
            for e in range(EXP_G)
            for i in range(pieces)
        ]
        for copy in copies:
            copy.start()
        for copy in copies:
            copy.wait()

    return call_small(
        kernel,
        jax.ShapeDtypeStruct(weights.shape, weights.dtype),
        (),
        [pltpu.SemaphoreType.DMA((EXP_G, pieces))],
        hbm=(weights,),
        cost=LOAD_COST,
        vmem_limit=vmem_limit,
    )


def unpack(blocks, unit):
    arrays = [array for array, _ in blocks]
    half = arrays[0].shape[1] - LANES

    def kernel(*refs):
        out_ref = refs[-1]
        values = [
            ref[number * unit : (number + 1) * unit, :].astype(f32)
            for ref, (_, number) in zip(refs[:-1], blocks, strict=True)
        ]
        pieces = []
        for i in (0, 2):
            a, b = unpack_pair(*values[i : i + 2])
            pieces.append((jnp.concatenate(a, 0), jnp.concatenate(b, 0)))
        rows_a, rows_b = (jnp.concatenate(part, 0) for part in zip(*pieces, strict=True))
        out_ref[:, :half] = rows_a[:, :half].astype(bf16)
        out_ref[:, half : 2 * half] = rows_b[:, :half].astype(bf16)
        out_ref[:, 2 * half :] = rows_a[:, half:].astype(bf16)

    shape = jax.ShapeDtypeStruct((len(blocks) * unit // 2, 2 * half + LANES), bf16)
    return call_small(kernel, shape, arrays)


def stack(arrays, *after):
    def kernel(*refs):
        at = 0
        for ref in refs[:-1]:
            refs[-1][at : at + ref.shape[0], :] = ref[...]
            at += ref.shape[0]

    rows = sum(a.shape[0] for a in arrays)
    return call_small(kernel, jax.ShapeDtypeStruct((rows, arrays[0].shape[1]), bf16), arrays, after=after)


def hold(block, *after, cost=None):
    return call_small(
        lambda block_ref, out_ref: out_ref.__setitem__(..., block_ref[...]),
        jax.ShapeDtypeStruct(block.shape, block.dtype),
        (block,),
        after=after,
        cost=cost or SMALL_COST,
    )


def expert_kernel(unit, far, count, *refs):
    blocks, refs = refs[:count], refs[count:]
    gate_ref, up_ref, down_ref, keep_far_ref, send_far_ref, keep_ref, send_ref = refs[:7]
    lhs_ref, hidden_ref, ring_ref, sems = refs[7:]
    width, depth = gate_ref.shape[1:]
    half = width // 2
    slots, column = ring_ref.shape[0], ring_ref.shape[2] // 2
    steps = [(chunk, expert) for chunk in range(half // column) for expert in range(EXP_G)]

    def fetch(step):
        chunk, expert = steps[step]
        return [
            pltpu.make_async_copy(
                down_ref.at[expert, :, pl.ds(side * half + chunk * column, column)],
                ring_ref.at[step % slots, :, pl.ds(side * column, column)],
                sems.at[step % slots, side],
            )
            for side in range(2)
        ]

    for step in range(slots):
        for copy in fetch(step):
            copy.start()
    group = lax.axis_index("wide") // (lax.axis_size("wide") // GROUPS)
    at = 0
    for ref in blocks:
        lhs_ref[at : at + ref.shape[0], :] = ref[:, :width]
        at += ref.shape[0]
    part = depth // GATE_CHUNKS

    def hidden_part(i, carry):
        expert = i // GATE_CHUNKS
        columns = pl.ds(pl.multiple_of(i % GATE_CHUNKS * part, part), part)
        gate_value = jnp.dot(lhs_ref[...], gate_ref[expert, :, columns], preferred_element_type=f32)
        lifted = jnp.dot(lhs_ref[...], up_ref[expert, :, columns], preferred_element_type=f32)
        scales = []
        for ref in blocks:
            route = ref[:, width:].astype(f32)
            lane = lax.broadcasted_iota(jnp.int32, route.shape, 1)
            scales.append(jnp.sum(jnp.where(lane == group * EXP_G + expert, route, 0.0), 1, keepdims=True))
        value = gate_value / (1.0 + jnp.exp(-gate_value)) * lifted * jnp.concatenate(scales, 0)
        hidden_ref[expert, :, columns] = value.astype(bf16)
        return carry

    lax.fori_loop(0, EXP_G * GATE_CHUNKS, hidden_part, 0)
    places = []
    for far_ref, ref in ((keep_far_ref, keep_ref), (send_far_ref, send_ref)):
        for first in range(0, far, 2):
            for near in range(2):
                for f in (first, first + 1):
                    places.append((far_ref, near) if f == far - 1 else (ref, near * (far - 1) + far - 2 - f))
    total = None
    for step, (chunk, expert) in enumerate(steps):
        for copy in fetch(step):
            copy.wait()
        part = jnp.dot(hidden_ref[expert], ring_ref[step % slots], preferred_element_type=f32)
        if step + slots < len(steps):
            for copy in fetch(step + slots):
                copy.start()
        if expert == 0:
            total = part
            continue
        total = total + part
        if expert < EXP_G - 1:
            continue
        columns = slice(chunk * column, (chunk + 1) * column)
        for pair in range(len(places) // 2):
            block = total[pair * unit : (pair + 1) * unit]
            packed = pack_pair(block[:, :column], block[:, column:])
            for (ref, place), parts in zip(places[2 * pair : 2 * pair + 2], packed, strict=True):
                ref[place * unit : (place + 1) * unit, columns] = jnp.concatenate(parts, 0).astype(bf16)


def expert_step(blocks, unit, w_gate, w_up, w_down):
    rows = sum(b.shape[0] for b in blocks)
    far = rows // unit // 2
    _, width, depth = w_up.shape
    half = width // 2
    column = half // DOWN_CHUNKS
    vmem = pl.BlockSpec(memory_space=pltpu.VMEM)
    few, many = (2 * unit, half), (2 * (far - 1) * unit, half)
    return pl.pallas_call(
        functools.partial(expert_kernel, unit, far, len(blocks)),
        out_shape=[jax.ShapeDtypeStruct(shape, bf16) for shape in (few, few, many, many)],
        in_specs=[vmem] * (len(blocks) + 2) + [pl.BlockSpec(memory_space=pl.ANY)],
        out_specs=[vmem] * 4,
        scratch_shapes=[
            pltpu.VMEM((rows, width), bf16),
            pltpu.VMEM((EXP_G, rows, depth), bf16),
            pltpu.VMEM((DOWN_RING, depth, 2 * column), bf16),
            pltpu.SemaphoreType.DMA((DOWN_RING, 2)),
        ],
        compiler_params=pltpu.CompilerParams(vmem_limit_bytes=STEP_VMEM),
        cost_estimate=STEP_COST,
    )(*blocks, w_gate, w_up, w_down)


def call_small(kernel, shapes, args, scratch=(), after=(), hbm=(), cost=SMALL_COST, vmem_limit=SMALL_VMEM):
    vmem = pl.BlockSpec(memory_space=pltpu.VMEM)
    count = len(args) + len(hbm)

    def body(*refs):
        kernel(*refs[:count], *refs[count + len(after) :])

    return pl.pallas_call(
        body,
        out_shape=shapes,
        in_specs=[vmem] * len(args) + [pl.BlockSpec(memory_space=pl.ANY)] * (len(hbm) + len(after)),
        out_specs=jax.tree.map(lambda _: vmem, shapes),
        scratch_shapes=list(scratch),
        compiler_params=pltpu.CompilerParams(vmem_limit_bytes=vmem_limit),
        cost_estimate=cost,
    )(*args, *hbm, *after)


def add_far(keep, got):
    unit = keep.shape[0] // 2

    def kernel(keep_ref, got_ref, mine_ref, near_ref):
        total = keep_ref[...].astype(f32) + got_ref[...].astype(f32)
        mine_ref[...] = total[:unit].astype(bf16)
        near_ref[...] = total[unit:].astype(bf16)

    return call_small(kernel, [jax.ShapeDtypeStruct((unit, keep.shape[1]), bf16)] * 2, (keep, got))


def add_rest(keep, got, unit, after):
    few = keep.shape[0] // (2 * unit)

    def kernel(keep_ref, got_ref, mine_ref, *near_refs):
        total = keep_ref[...].astype(f32) + got_ref[...].astype(f32)
        mine_ref[...] = total[: few * unit].astype(bf16)
        for i, ref in enumerate(near_refs):
            ref[...] = total[(few + i) * unit : (few + i + 1) * unit].astype(bf16)

    shapes = [jax.ShapeDtypeStruct((rows, keep.shape[1]), bf16) for rows in [few * unit] + [unit] * few]
    mine, *nears = call_small(kernel, shapes, (keep, got), after=after)
    return mine, nears


def add_one(keep, number, got, after=()):
    unit = got.shape[0]

    def kernel(keep_ref, got_ref, out_ref):
        kept = keep_ref[number * unit : (number + 1) * unit, :]
        out_ref[...] = (kept.astype(f32) + got_ref[...].astype(f32)).astype(bf16)

    return call_small(kernel, jax.ShapeDtypeStruct(got.shape, bf16), (keep, got), after=after)


def finish(keep, got, parts, rows):
    unit, half = got.shape
    padded = -(-rows // TILE) * TILE
    full = rows // TILE * TILE

    def kernel(keep_ref, *refs):
        out_ref, rows_ref = refs[-2:]
        total = keep_ref[keep_ref.shape[0] - unit :, :].astype(f32)
        for ref in refs[:-2]:
            total = total + ref[...].astype(f32)
        rest = total[2 * full :]
        rows_ref[:full, :half] = total[:full]
        rows_ref[:full, half:] = total[full : 2 * full]
        rows_ref[full:, :half] = rest
        rows_ref[full:, half:] = half_roll(rest)
        out_ref[...] = rows_ref[0:rows, :].astype(bf16)

    return call_small(
        kernel,
        jax.ShapeDtypeStruct((rows, 2 * half), bf16),
        (keep, got, *parts),
        [pltpu.VMEM((padded, 2 * half), f32)],
    )


def local(tokens, expert_ids, gates, w_gate, w_up, w_down):
    count = lax.axis_size("wide")
    far = count // 4
    rows, width = tokens.shape
    unit, half = 2 * rows, width // 2

    whole = prepare(tokens, expert_ids, gates)
    blocks = [whole] + [swap(whole, 4 * f, count) for f in range(1, far)]
    gate, up = w_gate, preload(w_up, FIRST_VMEM)
    pair = swap(stack(blocks[:2]), 2, count)
    nexts = [(pair, 0), (pair, 1)]
    nexts += [(swap(hold(block, up) if f == far - 2 else block, 2, count), 0) for f, block in enumerate(blocks) if f > 1]
    blocks = [(block, 0) for block in blocks]
    mine = [unpack(blocks[f : f + 2] + nexts[f : f + 2], unit) for f in range(0, far, 2)]
    other = [swap(rows_of, 1, count) for rows_of in mine]
    keep_far, send_far, keep, send = expert_step(mine + other, unit, gate, up, w_down)

    got = swap(send_far, 1, count)
    mine, near = add_far(keep_far, got)
    send = hold(send, got)
    got = swap(near, 2, count)
    last_far = hold(swap(add_one(mine, 0, got), 4 * (far - 1), count), cost=LOAD_COST)
    mine, nears = add_rest(keep, swap(send, 1, count), unit, [])
    parts = [last_far]
    for i, near in enumerate(nears):
        got = swap(near, 2, count)
        if i < far - 2:
            parts.append(swap(add_one(mine, i, got), 4 * (far - 2 - i), count))
    return finish(mine, got, parts, rows)


def solution(mesh):
    return jax.shard_map(
        local,
        mesh=mesh,
        in_specs=(
            P(("parts", "wide"), None),
            P(("parts", "wide"), None),
            P(("parts", "wide"), None),
            P(None, None, "wide"),
            P(None, None, "wide"),
            P(None, "wide", None),
        ),
        out_specs=P(("parts", "wide"), None),
        check_vma=False,
    )
```
